32 devices in a mesh: groups: 2 (over y), ep: 4 (over z), tp: 4 (over x, core).
Axes of the slice: x: 2, y: 2, z: 4, core: 2. Of those that a mesh axis runs over, the one named last changes fastest.
Arguments:
- latent_cache: bfloat16 [32, 576, 512], P(('groups', 'ep', 'tp')), parts along dimension 0, may hold values from -6 to 6
- queries: bfloat16 [32, 73728], P(('groups', 'ep'), 'tp'), parts along dimension 0, may hold values from -256 to 256
- destination: int32 [8, 4], P('groups'), parts along dimension 0, may hold values from 0 to 3, as said below
- cache_len: int32 [32], P(('groups', 'ep')), parts along dimension 0, may hold values from 64 to 512, as said below
- finished: int32 [32], P(('groups', 'ep')), parts along dimension 0, may hold values 0 or 1
- moe_input: bfloat16 [32, 7168], P(('groups', 'ep'), 'tp'), parts along dimension 0, may hold values from -6 to 6
- expert_ids: int32 [32, 8], P(('groups', 'ep')), parts along dimension 0, may hold values from 0 to 7, all different within a row; in each aligned block of 4 rows (0 to 3, 4 to 7, ...) at most 4 rows name the same one
- route_weight: bfloat16 [32, 8], P(('groups', 'ep')), parts along dimension 0, may hold values from 0.049804688 to 0.5
- up_weight: bfloat16 [8, 7168, 1024], P('ep', None, 'tp'), may hold values from -0.0625 to 0.0625
- down_weight: bfloat16 [8, 1024, 7168], P('ep', 'tp'), may hold values from -0.1875 to 0.1875
Outputs:
- moved_cache: bfloat16 [32, 576, 512], P(('groups', 'ep', 'tp')), parts along dimension 0
- context: bfloat16 [32, 65536], P(('groups', 'ep'), 'tp'), parts along dimension 0
- moe_out: bfloat16 [32, 7168], P(('groups', 'ep'), 'tp'), parts along dimension 0
The draws below stay inside these ranges and needn't reach their ends.
There are 2 independent parts, one for each index of `groups`. The reference program is written for one: setup_inputs(seed, part) draws one part's arguments, and reference() takes and returns one part's arrays. A program takes and returns all parts, laid end to end along the dimension named above; an argument that names none is the same for every part. Nothing has to cross between parts.
Inputs may be any that keep to these rules, and one draw needn't show every extreme that they name: Each column destination[:, t] is a permutation of the replicas. `cache_len`: some request has exactly 512 valid positions. `expert_ids`: the 8 experts of a token differ; among the 4 tokens of one replica no expert is named more than 4 times, a bound that some block reaches.
All inputs are finite; a program needn't handle non-finite values. No bound on the sum of `finished` on one device may be relied on, other than what follows from the above.
Results may differ from the reference program's by a relative error of at most 0.02.
Values may be sent and summed in bfloat16 or wider, within the bound.
A program may use at most 64 MiB of HBM per device.

```python
import math
import jax
import jax.numpy as jnp
import numpy as np
from jax import lax

D = 7168
HEADS = 128
LATENT = 512
HID = 1024
TOPK = 8
CAP = 4
CACHE_LEN = 512
LAT = 576
REPLICAS = 4
SLOTS = 4
REQ = 16
EXPERTS = 8
N_TP = 4


def migration_plan(key):
    key = jax.random.fold_in(key, 101)
    column_keys = jax.random.split(key, SLOTS)
    columns = jax.vmap(lambda single: jax.random.permutation(single, REPLICAS))(column_keys)
    return columns.T.astype(jnp.int32)


def request_lengths(key):
    key = jax.random.fold_in(key, 202)
    key_one, key_two = jax.random.split(key)
    shortest = max(4, CACHE_LEN // 8)
    sampled = jax.random.randint(key_one, (REQ,), shortest, CACHE_LEN + 1)
    longest = jax.random.randint(key_two, (), 0, REQ)
    return jnp.where(jnp.arange(REQ) == longest, CACHE_LEN, sampled).astype(jnp.int32)


def cache_values(key):
    key = jax.random.fold_in(key, 303)
    key_one = jax.random.fold_in(key, 0)
    gaussian = jnp.clip(jax.random.normal(key_one, (REQ, LAT, CACHE_LEN), jnp.float32), -6.0, 6.0)
    values = gaussian
    return values


def draw_destination(key, part):
    return migration_plan(key)


def draw_cache_len(key, part):
    return request_lengths(key)


def draw_latent_cache(key, part):
    values = cache_values(key)
    return values.astype(jnp.bfloat16)


def draw_queries(key, part):
    key = jax.random.fold_in(key, 404)
    result = jnp.clip(jax.random.normal(key, (REQ, HEADS, LAT), jnp.float32), -6.0, 6.0) * 0.5
    return result.reshape(REQ, HEADS * LAT).astype(jnp.bfloat16)


def touch_ends(drawn, rng, smallest, top_value):
    longest = drawn.shape.index(max(drawn.shape))
    spots = []
    for shift in (0, 1):
        where = [jax.random.randint(jax.random.fold_in(rng, axis), (), 0, length) for axis, length in enumerate(drawn.shape)]
        where[longest] = (where[longest] + shift) % drawn.shape[longest]
        spots.append(tuple(where))
    return drawn.at[spots[0]].set(smallest).at[spots[1]].set(top_value)


def steps_of(own_key, shape, shards, low, largest):
    def one(dim, parts):
        steps = jax.random.uniform(jax.random.fold_in(jax.random.fold_in(own_key, 6), dim), (parts,), jnp.float32, low / len(shards), largest / len(shards))
        return jnp.repeat(jnp.exp(steps), shape[dim] // parts).reshape((-1,) + (1,) * (len(shape) - dim - 1))

    gain = one(*shards[0])
    for cut in shards[1:]:
        gain = gain * one(*cut)
    return gain


def assign_block(key, own, number, rows, number_of, top, most, slope):
    order = jax.random.permutation(key, number_of)
    crowded, common = load_shares(number_of, rows * top, most, slope, True), load_shares(number_of, rows * top, most, slope, False)
    places = jnp.arange(number_of)

    def named(sizes, turn):
        used = int((sizes > 0).sum())
        fixed = max(1, used // 4)
        shifted = fixed + (places - fixed + turn * (used - fixed)) % max(1, number_of - fixed)
        return jnp.zeros((number_of,), jnp.int32).at[order[jnp.where(places < fixed, places, shifted)]].set(jnp.asarray(sizes, jnp.int32))

    sizes = jnp.where(number % 4 == 0, named(crowded, number // 4), named(common, number - number // 4 - 1))
    mixed = jax.random.permutation(jax.random.fold_in(own, 3), number_of)
    donor, sink = mixed[0:number_of // 2 * 2:2], mixed[1:number_of // 2 * 2:2]
    slack = jnp.minimum(sizes[donor] - 1, most - sizes[sink]) // 2
    slack = jnp.where((donor == order[0]) | (sink == order[0]) | (sizes[sink] == 0), 0, jnp.maximum(slack, 0))
    shifted = jax.random.randint(jax.random.fold_in(own, 4), (number_of // 2,), 0, 1 << 20) % (slack + 1)
    sizes = sizes.at[donor].add(-shifted).at[sink].add(shifted)
    labels = jnp.searchsorted(jnp.cumsum(sizes), jnp.arange(rows * top), side="right").astype(jnp.int32)
    grid = labels.reshape(top, rows).T
    grid = grid[jax.random.permutation(jax.random.fold_in(own, 1), rows)]
    turn = jax.random.randint(jax.random.fold_in(own, 2), (rows, 1), 0, top)
    return jnp.take_along_axis(grid, (jnp.arange(top)[None, :] + turn) % top, axis=1)


def load_shares(number_of, total, most, slope, full):
    portions = [(1 << 20) // math.isqrt(grade ** slope) + 1 for grade in range(1, number_of + 1)]
    largest = most if full else min(most, max(-(-total // number_of), total * portions[0] // sum(portions)))
    least = 1 if total - largest >= number_of - 1 else 0
    counts, spare = [largest] + [least] * (number_of - 1), total - largest - least * (number_of - 1)
    while spare > 0:
        movable = [i for i in range(1, number_of) if counts[i] < largest] or [i for i in range(1, number_of) if counts[i] < most]
        mass, budget = sum([portions[i] for i in movable]), spare
        for i in movable:
            more = min(most - counts[i], max(1, budget * portions[i] // mass), spare)
            counts[i] = counts[i] + more
            spare = spare - more
    return np.array(counts)


def normal_values(rng, dims, spread, limit, cuts=(), kind=jnp.bfloat16):
    gain = steps_of(rng, dims, cuts, -0.22, 0.18) if cuts else 1.0
    values = jax.random.normal(rng, dims, jnp.float32) * spread * gain
    return jnp.minimum(jnp.maximum(values, -limit), limit).astype(kind)


def setup_inputs(seed: int = 0, part: int = 0) -> dict:
    keys = jax.random.split(jax.random.key(seed), 11)
    part_keys = jax.random.split(jax.random.fold_in(keys[10], part), 11)
    latent_cache = draw_latent_cache(jax.random.fold_in(jax.random.fold_in(keys[10], part), 71), part)
    queries = draw_queries(jax.random.fold_in(jax.random.fold_in(keys[10], part), 71), part)
    destination = draw_destination(jax.random.fold_in(jax.random.fold_in(keys[10], part), 71), part)
    cache_len = draw_cache_len(jax.random.fold_in(jax.random.fold_in(keys[10], part), 71), part)
    finished = touch_ends((jax.random.randint(part_keys[4], (REQ,), 0, 8) < 1).astype(jnp.int32), jax.random.fold_in(part_keys[4], 1), 0, 1)
    moe_input = normal_values(part_keys[5], (REQ, D), 1.0, 6.0, ((0, 4), (1, 4)))
    expert_ids_keys = jax.random.split(jax.random.fold_in(part_keys[6], 1), REQ // SLOTS)
    expert_ids_turns = jax.random.permutation(jax.random.fold_in(part_keys[6], 3), REQ // SLOTS)
    expert_ids = jax.vmap(lambda own, number: assign_block(jax.random.fold_in(part_keys[6], 2), own, number, SLOTS, EXPERTS, TOPK, CAP, 2))(expert_ids_keys, expert_ids_turns).reshape((REQ, TOPK))
    route_weight = jnp.clip(jnp.exp(math.log(0.5) - 2.306499 * jax.random.uniform(part_keys[7], (REQ, TOPK), jnp.float32) ** steps_of(part_keys[7], (REQ, TOPK), ((0, 4),), -0.2, 0.2)), 0.049804688, 0.5).astype(jnp.bfloat16)
    up_weight = normal_values(keys[8], (EXPERTS, D, HID), D ** -0.5, 0.0625, ((0, 4), (2, 4)))
    down_weight = normal_values(keys[9], (EXPERTS, HID, D), HID ** -0.5, 0.1875, ((0, 4), (1, 4)))
    return dict(latent_cache=latent_cache, queries=queries, destination=destination, cache_len=cache_len, finished=finished, moe_input=moe_input, expert_ids=expert_ids, route_weight=route_weight, up_weight=up_weight, down_weight=down_weight)


score_scale = 192.0 ** -0.5


def reference(latent_cache, queries, destination, cache_len, finished, moe_input, expert_ids, route_weight, up_weight, down_weight):
    replica_rows = jnp.broadcast_to(jnp.arange(REPLICAS, dtype=jnp.int32)[:, None], (REPLICAS, SLOTS))
    slot_columns = jnp.broadcast_to(jnp.arange(SLOTS, dtype=jnp.int32)[None, :], (REPLICAS, SLOTS))
    root = jnp.zeros((REPLICAS, SLOTS), jnp.int32).at[destination, slot_columns].set(replica_rows)
    source = (root * SLOTS + slot_columns).reshape(REQ).astype(jnp.int32)
    moved_cache = jnp.take(latent_cache, source, axis=0)
    alive = finished == 0
    query_values = queries.reshape(REQ, HEADS, LAT).astype(jnp.float32)
    latents = moved_cache.astype(jnp.float32)
    scores = jnp.einsum("rhc,rcp->rhp", query_values, latents) * score_scale
    valid = jnp.arange(CACHE_LEN, dtype=jnp.int32)[None, None, :] < cache_len[:, None, None]
    scores = jnp.where(valid, scores, -jnp.inf)
    highest = jnp.max(scores, axis=2, keepdims=True)
    weights = jnp.exp(scores - highest)
    probabilities = (weights / jnp.sum(weights, axis=2, keepdims=True)).astype(jnp.bfloat16)
    attended = jnp.einsum("rhp,rcp->rhc", probabilities.astype(jnp.float32), latents[:, :LATENT, :])
    context = jnp.where(alive[:, None, None], attended, 0.0).astype(jnp.bfloat16).reshape(REQ, HEADS * LATENT)

    weighting = jnp.where(alive[:, None], route_weight.astype(jnp.float32), 0.0)
    group_width = HID // N_TP
    capacity = REPLICAS * CAP

    def one_expert(expert, total):
        matched = expert_ids == expert
        selected = jnp.any(matched, axis=1) & alive
        picked = jnp.sum(jnp.where(matched, weighting, 0.0), axis=1)
        chosen = jnp.nonzero(selected, size=capacity, fill_value=0)[0]
        live_count = jnp.sum(selected.astype(jnp.int32))
        token_rows = jnp.take(moe_input, chosen, axis=0)
        hidden = jax.nn.silu(jnp.dot(token_rows, up_weight[expert], preferred_element_type=jnp.float32)).astype(jnp.bfloat16)
        grouped = hidden.reshape(capacity, N_TP, group_width).astype(jnp.float32)
        down_block = down_weight[expert].reshape(N_TP, group_width, D).astype(jnp.float32)
        partials = jnp.einsum("sgk,gkd->gsd", grouped, down_block).astype(jnp.bfloat16)
        expert_out = jnp.sum(partials.astype(jnp.float32), axis=0).astype(jnp.bfloat16)
        in_use = jnp.arange(capacity) < live_count
        weight = jnp.where(in_use, jnp.take(picked, chosen), 0.0)
        return total.at[chosen].add(weight[:, None] * expert_out.astype(jnp.float32))

    total = lax.fori_loop(0, EXPERTS, one_expert, jnp.zeros((REQ, D), jnp.float32))
    moe_out = total.astype(jnp.bfloat16)
    return moved_cache, context, moe_out
```

```python
import functools

import jax
import jax.numpy as jnp
from jax import lax
from jax.experimental import pallas as pl
from jax.experimental.pallas import tpu as pltpu
from jax.sharding import PartitionSpec as P

MESH = pl.DeviceIdType.MESH
LATENT = 512
LANES = 128
PACK = 16

score_scale = 192.0 ** (-0.5)


def when(condition, body):
    if condition is None:
        body()
    else:
        pl.when(condition)(body)


def layer_kernel(
    replicas,
    slots,
    chunk,
    destination,
    cache_len,
    finished,
    latent_cache,
    queries,
    moe_input,
    expert_ids,
    route_weight,
    up_weight,
    down_weight,
    moved_cache,
    context,
    moe_out,
    up_block,
    down_block,
    message,
    messages,
    tokens,
    features,
    spread,
    ordered,
    moved,
    own_queries,
    attended,
    partials,
    arrived,
    totals,
    shares,
    returned,
    local_sem,
    message_send,
    message_recv,
    spread_send,
    spread_recv,
    ordered_send,
    ordered_recv,
    feature_send,
    feature_recv,
    query_send,
    query_recv,
    context_send,
    context_recv,
    partial_send,
    partial_recv,
    share_send,
    share_recv,
):
    ep = lax.axis_index("ep")
    tp = lax.axis_index("tp")
    width = moe_input.shape[1]
    experts_local = up_weight.shape[0]
    carriers = latent_cache.shape[0] // chunk
    heads_total = own_queries.shape[0] * own_queries.shape[1]

    def carries(i):
        return None if carriers == replicas else i < carriers

    def forth(axis, me, count, k):
        return lax.rem(me + k, count)

    def back(axis, me, count, k):
        return lax.rem(me + count - k, count)

    def rows(i):
        return pl.ds(pl.multiple_of(i * chunk, PACK), chunk)

    def remote(src, dst, send, recv, axis, target):
        return pltpu.make_async_remote_copy(
            src_ref=src,
            dst_ref=dst,
            send_sem=send,
            recv_sem=recv,
            device_id={axis: target},
            device_id_type=MESH,
        )

    up_copy = pltpu.make_async_copy(up_weight, up_block, local_sem.at[0])
    down_copy = pltpu.make_async_copy(down_weight, down_block, local_sem.at[1])
    query_copy = pltpu.make_async_copy(queries.at[tp], own_queries.at[tp], local_sem.at[2])
    own_chunk = pltpu.make_async_copy(
        latent_cache.at[rows(ep if carriers == replicas else lax.rem(ep, carriers))],
        spread.at[ep],
        local_sem.at[3],
    )
    up_copy.start()
    down_copy.start()
    query_copy.start()
    own_chunk.start()

    lane = lax.broadcasted_iota(jnp.int32, (slots, LANES), 1)
    token = lax.broadcasted_iota(jnp.int32, (slots, LANES), 0)
    table = jnp.zeros((slots, LANES), jnp.float32)
    ids = expert_ids[...]
    weights = route_weight[...].astype(jnp.float32)
    for k in range(ids.shape[1]):
        table += jnp.where(ids[:, k : k + 1] == lane, weights[:, k : k + 1], 0.0)
    for s in range(slots):
        table = jnp.where((token == s) & (finished[s] != 0), 0.0, table)
    message[:, :width] = moe_input[...]
    message[:, width:] = table.astype(jnp.bfloat16)

    barrier = pltpu.get_barrier_semaphore()
    for k in range(1, replicas):
        pl.semaphore_signal(
            barrier, inc=1, device_id={"ep": lax.rem(ep + k, replicas)}, device_id_type=MESH
        )
    for k in range(1, slots):
        pl.semaphore_signal(
            barrier, inc=1, device_id={"tp": lax.rem(tp + k, slots)}, device_id_type=MESH
        )
    pl.semaphore_wait(barrier, replicas + slots - 2)

    def message_to(k):
        return remote(
            message, messages.at[ep], message_send.at[k], message_recv.at[k],
            "ep", lax.rem(ep + k, replicas),
        )

    def chunk_to(k):
        target = lax.rem(ep + k, replicas)
        return remote(
            latent_cache.at[rows(target)], spread.at[ep], spread_send.at[k], spread_recv.at[k],
            "ep", target,
        )

    def queries_to(k):
        target = lax.rem(tp + k, slots)
        return remote(
            queries.at[target], own_queries.at[tp], query_send.at[k], query_recv.at[k],
            "tp", target,
        )

    for k in range(1, replicas):
        message_to(k).start()
    for k in range(1, replicas):
        when(carries(lax.rem(ep + k, replicas)), lambda: chunk_to(k).start())
    for k in range(1, slots):
        queries_to(k).start()

    messages[ep] = message[...]
    for k in range(1, replicas):
        message_to(k).wait_recv()
    for r in range(replicas):
        tokens[r * slots : (r + 1) * slots, :] = messages[r].astype(jnp.float32)
    features[tp] = tokens[:, :width].astype(jnp.bfloat16)

    def features_to(k):
        return remote(
            features.at[tp], features.at[tp], feature_send.at[k], feature_recv.at[k],
            "tp", lax.rem(tp + k, slots),
        )

    for k in range(1, slots):
        features_to(k).start()

    def ordered_to(k):
        target = lax.rem(ep + k, replicas)
        return remote(
            ordered.at[target], moved.at[rows(ep)], ordered_send.at[k], ordered_recv.at[k],
            "ep", target,
        )

    def reorder():
        for k in range(1, replicas):
            chunk_to(k).wait_recv()
        def root_of(target):
            root = jnp.int32(0)
            for o in range(replicas):
                root = jnp.where(destination[o, tp] == target, jnp.int32(o), root)
            return root
        for k in range(1, replicas):
            target = lax.rem(ep + k, replicas)
            ordered[target] = spread[root_of(target)]
            ordered_to(k).start()
        moved[rows(ep), :] = spread[root_of(ep)]

    own_chunk.wait()
    when(carries(ep), reorder)

    for k in range(1, slots):
        features_to(k).wait_recv()
    up_copy.wait()
    down_copy.wait()
    all_weights = tokens[:, width:]
    all_lanes = lax.broadcasted_iota(jnp.int32, all_weights.shape, 1)
    weighted = []
    for j in range(experts_local):
        raised = None
        for t in range(slots):
            term = jnp.dot(
                features[t],
                up_block[j, t * width : (t + 1) * width, :],
                preferred_element_type=jnp.float32,
            )
            raised = term if raised is None else raised + term
        hidden = (raised / (1.0 + jnp.exp(-raised))).astype(jnp.bfloat16).astype(jnp.float32)
        column = jnp.sum(
            jnp.where(all_lanes == ep * experts_local + j, all_weights, 0.0), axis=1, keepdims=True
        )
        weighted.append((hidden * column).astype(jnp.bfloat16))
    for t in range(slots):
        total = None
        for j in range(experts_local):
            term = jnp.dot(
                weighted[j],
                down_block[j, :, t * width : (t + 1) * width],
                preferred_element_type=jnp.float32,
            )
            total = term if total is None else total + term
        partials[t] = total.astype(jnp.bfloat16)

    def partial_to(k):
        target = lax.rem(tp + k, slots)
        return remote(
            partials.at[target], arrived.at[tp], partial_send.at[k], partial_recv.at[k],
            "tp", target,
        )

    for k in range(1, slots):
        partial_to(k).start()

    totals[...] = partials[tp].astype(jnp.float32)
    for k in range(1, slots):
        partial_to(k).wait_recv()
        totals[...] += arrived[lax.rem(tp + slots - k, slots)].astype(jnp.float32)
    for r in range(replicas):
        shares[r] = totals[r * slots : (r + 1) * slots, :].astype(jnp.bfloat16)

    def share_to(k):
        target = lax.rem(ep + k, replicas)
        return remote(
            shares.at[target], returned.at[ep], share_send.at[k], share_recv.at[k],
            "ep", target,
        )

    for k in range(1, replicas):
        share_to(k).start()

    query_copy.wait()
    for k in range(1, slots):
        queries_to(k).wait_recv()
    for k in range(1, replicas):
        source = lax.rem(ep + replicas - k, replicas)
        arrival = remote(
            ordered.at[0], moved.at[rows(source)], ordered_send.at[k], ordered_recv.at[k],
            "ep", source,
        )
        when(carries(source), lambda: arrival.wait_recv())
    moved_copy = pltpu.make_async_copy(moved, moved_cache, local_sem.at[4])
    moved_copy.start()
    cache = moved[...]
    query_block = own_queries[...].reshape(heads_total, latent_cache.shape[0])
    scores = jnp.dot(query_block, cache, preferred_element_type=jnp.float32) * score_scale
    positions = lax.broadcasted_iota(jnp.int32, scores.shape, 1)
    scores = jnp.where(positions < cache_len[tp], scores, -jnp.inf)
    highest = jnp.max(scores, axis=1, keepdims=True)
    exps = jnp.exp(scores - highest)
    probabilities = (exps / jnp.sum(exps, axis=1, keepdims=True)).astype(jnp.bfloat16)
    result = lax.dot_general(
        probabilities, cache[:LATENT, :], (((1,), (1,)), ((), ())),
        preferred_element_type=jnp.float32,
    )
    result = jnp.where(finished[tp] == 0, result, 0.0).astype(jnp.bfloat16)
    attended[...] = result.reshape(attended.shape)

    def context_to(k):
        target = lax.rem(tp + k, slots)
        return remote(
            attended.at[target], context.at[tp], context_send.at[k], context_recv.at[k],
            "tp", target,
        )

    for k in range(1, slots):
        context_to(k).start()
    own_context = pltpu.make_async_copy(attended.at[tp], context.at[tp], local_sem.at[5])
    own_context.start()

    result = shares[ep].astype(jnp.float32)
    for k in range(1, replicas):
        share_to(k).wait_recv()
        result += returned[lax.rem(ep + replicas - k, replicas)].astype(jnp.float32)
    moe_out[...] = result.astype(jnp.bfloat16)

    for k in range(1, slots):
        context_to(k).wait_recv()
    own_context.wait()
    moved_copy.wait()
    for k in range(1, replicas):
        message_to(k).wait_send()
        share_to(k).wait_send()
        when(carries(lax.rem(ep + k, replicas)), lambda: chunk_to(k).wait_send())
        when(carries(ep), lambda: ordered_to(k).wait_send())
    for k in range(1, slots):
        queries_to(k).wait_send()
        features_to(k).wait_send()
        partial_to(k).wait_send()
        context_to(k).wait_send()


def shards(
    latent_cache,
    queries,
    destination,
    cache_len,
    finished,
    moe_input,
    expert_ids,
    route_weight,
    up_weight,
    down_weight,
):
    replicas = lax.axis_size("ep")
    slots = lax.axis_size("tp")
    latent_width, length = latent_cache.shape[1:]
    heads = queries.shape[1] // latent_width
    width = moe_input.shape[1]
    chunk = -(-(latent_width // replicas) // PACK) * PACK
    everyone = replicas * slots
    bf16, f32 = jnp.bfloat16, jnp.float32
    dma = pltpu.SemaphoreType.DMA
    anywhere = pl.BlockSpec(memory_space=pl.ANY)
    scalars = pl.BlockSpec(memory_space=pltpu.SMEM)
    near = pl.BlockSpec(memory_space=pltpu.VMEM)
    moved_cache, context, moe_out = pl.pallas_call(
        functools.partial(layer_kernel, replicas, slots, chunk),
        out_shape=(
            jax.ShapeDtypeStruct((latent_width, length), bf16),
            jax.ShapeDtypeStruct((slots, heads, LATENT), bf16),
            jax.ShapeDtypeStruct((slots, width), bf16),
        ),
        in_specs=[scalars] * 3 + [anywhere] * 2 + [near] * 3 + [anywhere] * 2,
        out_specs=(anywhere, anywhere, near),
        scratch_shapes=[
            pltpu.VMEM(up_weight.shape, bf16),
            pltpu.VMEM(down_weight.shape, bf16),
            pltpu.VMEM((slots, width + LANES), bf16),
            pltpu.VMEM((replicas, slots, width + LANES), bf16),
            pltpu.VMEM((everyone, width + LANES), f32),
            pltpu.VMEM((slots, everyone, width), bf16),
            pltpu.VMEM((replicas, chunk, length), bf16),
            pltpu.VMEM((replicas, chunk, length), bf16),
            pltpu.VMEM((latent_width, length), bf16),
            pltpu.VMEM((slots, heads, latent_width), bf16),
            pltpu.VMEM((slots, heads, LATENT), bf16),
            pltpu.VMEM((slots, everyone, width), bf16),
            pltpu.VMEM((slots, everyone, width), bf16),
            pltpu.VMEM((everyone, width), f32),
            pltpu.VMEM((replicas, slots, width), bf16),
            pltpu.VMEM((replicas, slots, width), bf16),
            dma((6,)),
            dma((replicas,)),
            dma((replicas,)),
            dma((replicas,)),
            dma((replicas,)),
            dma((replicas,)),
            dma((replicas,)),
            dma((slots,)),
            dma((slots,)),
            dma((slots,)),
            dma((slots,)),
            dma((slots,)),
            dma((slots,)),
            dma((slots,)),
            dma((slots,)),
            dma((replicas,)),
            dma((replicas,)),
        ],
        compiler_params=pltpu.CompilerParams(
            collective_id=0, has_side_effects=True, vmem_limit_bytes=44 * 1024 * 1024
        ),
    )(
        destination,
        cache_len,
        finished,
        latent_cache.reshape(latent_width, length),
        queries.reshape(slots, heads, latent_width),
        moe_input,
        expert_ids,
        route_weight,
        up_weight,
        down_weight,
    )
    return (
        moved_cache.reshape(1, latent_width, length),
        context.reshape(slots, heads * LATENT),
        moe_out,
    )


def solution(mesh):
    return jax.shard_map(
        shards,
        mesh=mesh,
        in_specs=(
            P(("groups", "ep", "tp"), None, None),
            P(("groups", "ep"), "tp"),
            P("groups", None),
            P(("groups", "ep")),
            P(("groups", "ep")),
            P(("groups", "ep"), "tp"),
            P(("groups", "ep"), None),
            P(("groups", "ep"), None),
            P("ep", None, "tp"),
            P("ep", "tp", None),
        ),
        out_specs=(
            P(("groups", "ep", "tp"), None, None),
            P(("groups", "ep"), "tp"),
            P(("groups", "ep"), "tp"),
        ),
        check_vma=False,
    )
```

```python
import functools

import jax
import jax.numpy as jnp
from jax import lax
from jax.experimental import pallas as pl
from jax.experimental.pallas import tpu as pltpu
from jax.sharding import PartitionSpec as P

MESH = pl.DeviceIdType.MESH
LATENT = 512
LANES = 128
PACK = 16

score_scale = 192.0 ** (-0.5)


def when(condition, body):
    if condition is None:
        body()
    else:
        pl.when(condition)(body)


def layer_kernel(
    replicas,
    slots,
    chunk,
    destination,
    cache_len,
    finished,
    latent_cache,
    queries,
    moe_input,
    expert_ids,
    route_weight,
    up_weight,
    down_weight,
    moved_cache,
    context,
    moe_out,
    plan,
    lengths,
    ended,
    input_block,
    id_block,
    route_block,
    up_block,
    down_block,
    message,
    messages,
    tokens,
    features,
    spread,
    ordered,
    moved,
    own_queries,
    attended,
    partials,
    arrived,
    totals,
    shares,
    returned,
    local_sem,
    message_send,
    message_recv,
    spread_send,
    spread_recv,
    ordered_send,
    ordered_recv,
    feature_send,
    feature_recv,
    query_send,
    query_recv,
    context_send,
    context_recv,
    partial_send,
    partial_recv,
    share_send,
    share_recv,
):
    ep = lax.axis_index("ep")
    tp = lax.axis_index("tp")
    width = moe_input.shape[1]
    experts_local = up_weight.shape[0]
    carriers = latent_cache.shape[0] // chunk
    heads_total = own_queries.shape[0] * own_queries.shape[1]

    def carries(i):
        return None if carriers == replicas else i < carriers

    def forth(axis, me, count, k):
        return lax.rem(me + k, count)

    def back(axis, me, count, k):
        return lax.rem(me + count - k, count)

    def rows(i):
        return pl.ds(pl.multiple_of(i * chunk, PACK), chunk)

    def remote(src, dst, send, recv, axis, target):
        return pltpu.make_async_remote_copy(
            src_ref=src,
            dst_ref=dst,
            send_sem=send,
            recv_sem=recv,
            device_id={axis: target},
            device_id_type=MESH,
        )

    barrier = pltpu.get_barrier_semaphore()
    for k in range(1, replicas):
        pl.semaphore_signal(
            barrier, inc=1, device_id={"ep": lax.rem(ep + k, replicas)}, device_id_type=MESH
        )
    for k in range(1, slots):
        pl.semaphore_signal(
            barrier, inc=1, device_id={"tp": lax.rem(tp + k, slots)}, device_id_type=MESH
        )

    up_copy = pltpu.make_async_copy(up_weight, up_block, local_sem.at[0])
    down_copy = pltpu.make_async_copy(down_weight, down_block, local_sem.at[1])
    query_copy = pltpu.make_async_copy(queries.at[tp], own_queries.at[tp], local_sem.at[2])
    own_chunk = pltpu.make_async_copy(
        latent_cache.at[rows(ep if carriers == replicas else lax.rem(ep, carriers))],
        spread.at[ep],
        local_sem.at[3],
    )
    small = [
        pltpu.make_async_copy(src, dst, local_sem.at[6 + i])
        for i, (src, dst) in enumerate(
            (
                (moe_input, input_block),
                (expert_ids, id_block),
                (route_weight, route_block),
                (finished, ended),
                (destination, plan),
                (cache_len, lengths),
            )
        )
    ]
    for copy in small:
        copy.start()
    query_copy.start()
    own_chunk.start()

    lane = lax.broadcasted_iota(jnp.int32, (slots, LANES), 1)
    token = lax.broadcasted_iota(jnp.int32, (slots, LANES), 0)
    table = jnp.zeros((slots, LANES), jnp.float32)
    for copy in small:
        copy.wait()
    ids = id_block[...]
    weights = route_block[...].astype(jnp.float32)
    for k in range(ids.shape[1]):
        table += jnp.where(ids[:, k : k + 1] == lane, weights[:, k : k + 1], 0.0)
    for s in range(slots):
        table = jnp.where((token == s) & (ended[s] != 0), 0.0, table)
    message[:, :width] = input_block[...]
    message[:, width:] = table.astype(jnp.bfloat16)

    pl.semaphore_wait(barrier, replicas + slots - 2)

    up_copy.start()
    down_copy.start()

    def message_to(k):
        return remote(
            message, messages.at[ep], message_send.at[k], message_recv.at[k],
            "ep", lax.rem(ep + k, replicas),
        )

    def chunk_to(k):
        target = lax.rem(ep + k, replicas)
        return remote(
            latent_cache.at[rows(target)], spread.at[ep], spread_send.at[k], spread_recv.at[k],
            "ep", target,
        )

    def queries_to(k):
        target = lax.rem(tp + k, slots)
        return remote(
            queries.at[target], own_queries.at[tp], query_send.at[k], query_recv.at[k],
            "tp", target,
        )

    for k in range(1, replicas):
        message_to(k).start()
    for k in range(1, replicas):
        when(carries(lax.rem(ep + k, replicas)), lambda: chunk_to(k).start())
    for k in range(1, slots):
        queries_to(k).start()

    messages[ep] = message[...]
    for k in range(1, replicas):
        message_to(k).wait_recv()
    for r in range(replicas):
        tokens[r * slots : (r + 1) * slots, :] = messages[r].astype(jnp.float32)
    features[tp] = tokens[:, :width].astype(jnp.bfloat16)

    def features_to(k):
        return remote(
            features.at[tp], features.at[tp], feature_send.at[k], feature_recv.at[k],
            "tp", lax.rem(tp + k, slots),
        )

    for k in range(1, slots):
        features_to(k).start()

    def ordered_to(k):
        target = lax.rem(ep + k, replicas)
        return remote(
            ordered.at[target], moved.at[rows(ep)], ordered_send.at[k], ordered_recv.at[k],
            "ep", target,
        )

    def reorder():
        for k in range(1, replicas):
            chunk_to(k).wait_recv()
        def root_of(target):
            root = jnp.int32(0)
            for o in range(replicas):
                root = jnp.where(plan[o, tp] == target, jnp.int32(o), root)
            return root
        for k in range(1, replicas):
            target = lax.rem(ep + k, replicas)
            ordered[target] = spread[root_of(target)]
            ordered_to(k).start()
        moved[rows(ep), :] = spread[root_of(ep)]

    own_chunk.wait()
    when(carries(ep), reorder)

    for k in range(1, slots):
        features_to(k).wait_recv()
    up_copy.wait()
    down_copy.wait()
    all_weights = tokens[:, width:]
    all_lanes = lax.broadcasted_iota(jnp.int32, all_weights.shape, 1)
    weighted = []
    for j in range(experts_local):
        raised = None
        for t in range(slots):
            term = jnp.dot(
                features[t],
                up_block[j, t * width : (t + 1) * width, :],
                preferred_element_type=jnp.float32,
            )
            raised = term if raised is None else raised + term
        hidden = (raised / (1.0 + jnp.exp(-raised))).astype(jnp.bfloat16).astype(jnp.float32)
        column = jnp.sum(
            jnp.where(all_lanes == ep * experts_local + j, all_weights, 0.0), axis=1, keepdims=True
        )
        weighted.append((hidden * column).astype(jnp.bfloat16))
    for t in range(slots):
        total = None
        for j in range(experts_local):
            term = jnp.dot(
                weighted[j],
                down_block[j, :, t * width : (t + 1) * width],
                preferred_element_type=jnp.float32,
            )
            total = term if total is None else total + term
        partials[t] = total.astype(jnp.bfloat16)

    def partial_to(k):
        target = lax.rem(tp + k, slots)
        return remote(
            partials.at[target], arrived.at[tp], partial_send.at[k], partial_recv.at[k],
            "tp", target,
        )

    for k in range(1, slots):
        partial_to(k).start()

    totals[...] = partials[tp].astype(jnp.float32)
    for k in range(1, slots):
        partial_to(k).wait_recv()
        totals[...] += arrived[lax.rem(tp + slots - k, slots)].astype(jnp.float32)
    for r in range(replicas):
        shares[r] = totals[r * slots : (r + 1) * slots, :].astype(jnp.bfloat16)

    def share_to(k):
        target = lax.rem(ep + k, replicas)
        return remote(
            shares.at[target], returned.at[ep], share_send.at[k], share_recv.at[k],
            "ep", target,
        )

    for k in range(1, replicas):
        share_to(k).start()

    query_copy.wait()
    for k in range(1, slots):
        queries_to(k).wait_recv()
    for k in range(1, replicas):
        source = lax.rem(ep + replicas - k, replicas)
        arrival = remote(
            ordered.at[0], moved.at[rows(source)], ordered_send.at[k], ordered_recv.at[k],
            "ep", source,
        )
        when(carries(source), lambda: arrival.wait_recv())
    moved_copy = pltpu.make_async_copy(moved, moved_cache, local_sem.at[4])
    moved_copy.start()
    cache = moved[...]
    query_block = own_queries[...].reshape(heads_total, latent_cache.shape[0])
    scores = jnp.dot(query_block, cache, preferred_element_type=jnp.float32) * score_scale
    positions = lax.broadcasted_iota(jnp.int32, scores.shape, 1)
    scores = jnp.where(positions < lengths[tp], scores, -jnp.inf)
    highest = jnp.max(scores, axis=1, keepdims=True)
    exps = jnp.exp(scores - highest)
    probabilities = (exps / jnp.sum(exps, axis=1, keepdims=True)).astype(jnp.bfloat16)
    result = lax.dot_general(
        probabilities, cache[:LATENT, :], (((1,), (1,)), ((), ())),
        preferred_element_type=jnp.float32,
    )
    result = jnp.where(ended[tp] == 0, result, 0.0).astype(jnp.bfloat16)
    attended[...] = result.reshape(attended.shape)

    def context_to(k):
        target = lax.rem(tp + k, slots)
        return remote(
            attended.at[target], context.at[tp], context_send.at[k], context_recv.at[k],
            "tp", target,
        )

    for k in range(1, slots):
        context_to(k).start()
    own_context = pltpu.make_async_copy(attended.at[tp], context.at[tp], local_sem.at[5])
    own_context.start()

    result = shares[ep].astype(jnp.float32)
    for k in range(1, replicas):
        share_to(k).wait_recv()
        result += returned[lax.rem(ep + replicas - k, replicas)].astype(jnp.float32)
    moe_out[...] = result.astype(jnp.bfloat16)

    for k in range(1, slots):
        context_to(k).wait_recv()
    own_context.wait()
    moved_copy.wait()
    for k in range(1, replicas):
        message_to(k).wait_send()
        share_to(k).wait_send()
        when(carries(lax.rem(ep + k, replicas)), lambda: chunk_to(k).wait_send())
        when(carries(ep), lambda: ordered_to(k).wait_send())
    for k in range(1, slots):
        queries_to(k).wait_send()
        features_to(k).wait_send()
        partial_to(k).wait_send()
        context_to(k).wait_send()


def shards(
    latent_cache,
    queries,
    destination,
    cache_len,
    finished,
    moe_input,
    expert_ids,
    route_weight,
    up_weight,
    down_weight,
):
    replicas = lax.axis_size("ep")
    slots = lax.axis_size("tp")
    latent_width, length = latent_cache.shape[1:]
    heads = queries.shape[1] // latent_width
    width = moe_input.shape[1]
    chunk = -(-(latent_width // replicas) // PACK) * PACK
    everyone = replicas * slots
    bf16, f32 = jnp.bfloat16, jnp.float32
    dma = pltpu.SemaphoreType.DMA
    anywhere = pl.BlockSpec(memory_space=pl.ANY)
    far = pl.BlockSpec(memory_space=pltpu.HBM)
    near = pl.BlockSpec(memory_space=pltpu.VMEM)
    moved_cache, context, moe_out = pl.pallas_call(
        functools.partial(layer_kernel, replicas, slots, chunk),
        out_shape=(
            jax.ShapeDtypeStruct((latent_width, length), bf16),
            jax.ShapeDtypeStruct((slots, heads, LATENT), bf16),
            jax.ShapeDtypeStruct((slots, width), bf16),
        ),
        in_specs=[far] * 10,
        out_specs=(anywhere, anywhere, near),
        scratch_shapes=[
            pltpu.SMEM(destination.shape, jnp.int32),
            pltpu.SMEM(cache_len.shape, jnp.int32),
            pltpu.SMEM(finished.shape, jnp.int32),
            pltpu.VMEM(moe_input.shape, bf16),
            pltpu.VMEM(expert_ids.shape, jnp.int32),
            pltpu.VMEM(route_weight.shape, bf16),
            pltpu.VMEM(up_weight.shape, bf16),
            pltpu.VMEM(down_weight.shape, bf16),
            pltpu.VMEM((slots, width + LANES), bf16),
            pltpu.VMEM((replicas, slots, width + LANES), bf16),
            pltpu.VMEM((everyone, width + LANES), f32),
            pltpu.VMEM((slots, everyone, width), bf16),
            pltpu.VMEM((replicas, chunk, length), bf16),
            pltpu.VMEM((replicas, chunk, length), bf16),
            pltpu.VMEM((latent_width, length), bf16),
            pltpu.VMEM((slots, heads, latent_width), bf16),
            pltpu.VMEM((slots, heads, LATENT), bf16),
            pltpu.VMEM((slots, everyone, width), bf16),
            pltpu.VMEM((slots, everyone, width), bf16),
            pltpu.VMEM((everyone, width), f32),
            pltpu.VMEM((replicas, slots, width), bf16),
            pltpu.VMEM((replicas, slots, width), bf16),
            dma((12,)),
            dma((replicas,)),
            dma((replicas,)),
            dma((replicas,)),
            dma((replicas,)),
            dma((replicas,)),
            dma((replicas,)),
            dma((slots,)),
            dma((slots,)),
            dma((slots,)),
            dma((slots,)),
            dma((slots,)),
            dma((slots,)),
            dma((slots,)),
            dma((slots,)),
            dma((replicas,)),
            dma((replicas,)),
        ],
        compiler_params=pltpu.CompilerParams(
            collective_id=0, has_side_effects=True, vmem_limit_bytes=56 * 1024 * 1024
        ),
    )(
        destination,
        cache_len,
        finished,
        latent_cache.reshape(latent_width, length),
        queries.reshape(slots, heads, latent_width),
        moe_input,
        expert_ids,
        route_weight,
        up_weight,
        down_weight,
    )
    return (
        moved_cache.reshape(1, latent_width, length),
        context.reshape(slots, heads * LATENT),
        moe_out,
    )


def solution(mesh):
    return jax.shard_map(
        shards,
        mesh=mesh,
        in_specs=(
            P(("groups", "ep", "tp"), None, None),
            P(("groups", "ep"), "tp"),
            P("groups", None),
            P(("groups", "ep")),
            P(("groups", "ep")),
            P(("groups", "ep"), "tp"),
            P(("groups", "ep"), None),
            P(("groups", "ep"), None),
            P("ep", None, "tp"),
            P("ep", "tp", None),
        ),
        out_specs=(
            P(("groups", "ep", "tp"), None, None),
            P(("groups", "ep"), "tp"),
            P(("groups", "ep"), "tp"),
        ),
        check_vma=False,
    )
```

```python
import functools

import jax
import jax.numpy as jnp
from jax import lax
from jax.experimental import pallas as pl
from jax.experimental.pallas import tpu as pltpu
from jax.sharding import PartitionSpec as P

MESH = pl.DeviceIdType.MESH
LATENT = 512
LANES = 128
PACK = 16
VMEM_BYTES = 56 * 1024 * 1024

score_scale = 192.0 ** (-0.5)


def when(condition, body):
    if condition is None:
        body()
    else:
        pl.when(condition)(body)


def layer_kernel(
    replicas,
    slots,
    chunk,
    piece,
    destination,
    cache_len,
    finished,
    latent_cache,
    queries,
    moe_input,
    expert_ids,
    route_weight,
    up_weight,
    down_weight,
    moved_cache,
    context,
    moe_out,
    plan,
    lengths,
    ended,
    input_block,
    id_block,
    route_block,
    up_block,
    down_block,
    message,
    messages,
    tokens,
    features,
    spread,
    ordered,
    moved,
    query_rows,
    query_heads,
    sent_queries,
    own_queries,
    attended,
    partials,
    arrived,
    totals,
    shares,
    returned,
    summed,
    local_sem,
    own_sem,
    message_send,
    message_recv,
    spread_send,
    spread_recv,
    ordered_send,
    ordered_recv,
    feature_send,
    feature_recv,
    query_send,
    query_recv,
    context_send,
    context_recv,
    partial_send,
    partial_recv,
    share_send,
    share_recv,
):
    ep = lax.axis_index("ep")
    tp = lax.axis_index("tp")
    width = moe_input.shape[1]
    experts_local = up_weight.shape[0]
    carriers = latent_cache.shape[0] // chunk
    pieces = chunk // piece
    heads_total = own_queries.shape[0] * own_queries.shape[1]

    def carries(i):
        return None if carriers == replicas else i < carriers

    def forth(axis, me, count, k):
        return lax.rem(me + k, count)

    def back(axis, me, count, k):
        return lax.rem(me + count - k, count)

    def rows(i, p):
        return pl.ds(pl.multiple_of(i * chunk + p * piece, PACK), piece)

    def part(p):
        return pl.ds(p * piece, piece)

    def remote(src, dst, send, recv, axis, target):
        return pltpu.make_async_remote_copy(
            src_ref=src,
            dst_ref=dst,
            send_sem=send,
            recv_sem=recv,
            device_id={axis: target},
            device_id_type=MESH,
        )

    barrier = pltpu.get_barrier_semaphore()
    for k in range(1, replicas):
        pl.semaphore_signal(
            barrier, inc=1, device_id={"ep": lax.rem(ep + k, replicas)}, device_id_type=MESH
        )
    for k in range(1, slots):
        pl.semaphore_signal(
            barrier, inc=1, device_id={"tp": lax.rem(tp + k, slots)}, device_id_type=MESH
        )

    up_copy = pltpu.make_async_copy(up_weight, up_block, local_sem.at[0])
    down_copy = pltpu.make_async_copy(down_weight, down_block, local_sem.at[1])
    query_copy = pltpu.make_async_copy(queries, query_rows, local_sem.at[2])
    own_chunk = [
        pltpu.make_async_copy(
            latent_cache.at[rows(ep if carriers == replicas else lax.rem(ep, carriers), p)],
            spread[p].at[ep],
            own_sem.at[p],
        )
        for p in range(pieces)
    ]
    small = [
        pltpu.make_async_copy(src, dst, local_sem.at[6 + i])
        for i, (src, dst) in enumerate(
            (
                (moe_input, input_block),
                (expert_ids, id_block),
                (route_weight, route_block),
                (finished, ended),
                (destination, plan),
                (cache_len, lengths),
            )
        )
    ]
    for copy in small:
        copy.start()
    query_copy.start()
    for copy in own_chunk:
        copy.start()

    lane = lax.broadcasted_iota(jnp.int32, (slots, LANES), 1)
    token = lax.broadcasted_iota(jnp.int32, (slots, LANES), 0)
    table = jnp.zeros((slots, LANES), jnp.float32)
    for copy in small:
        copy.wait()
    ids = id_block[...]
    weights = route_block[...].astype(jnp.float32)
    for k in range(ids.shape[1]):
        table += jnp.where(ids[:, k : k + 1] == lane, weights[:, k : k + 1], 0.0)
    for s in range(slots):
        table = jnp.where((token == s) & (ended[s] != 0), 0.0, table)
    message[:, :width] = input_block[...]
    message[:, width:] = table.astype(jnp.bfloat16)

    pl.semaphore_wait(barrier, replicas + slots - 2)

    up_copy.start()
    down_copy.start()

    def message_to(k):
        return remote(
            message, messages.at[ep], message_send.at[k], message_recv.at[k],
            "ep", lax.rem(ep + k, replicas),
        )

    def chunk_to(p, k):
        target = lax.rem(ep + k, replicas)
        return remote(
            latent_cache.at[rows(target, p)], spread[p].at[ep],
            spread_send.at[p, k], spread_recv.at[p, k], "ep", target,
        )

    def queries_to(k):
        target = lax.rem(tp + k, slots)
        return remote(
            sent_queries.at[target], own_queries.at[tp], query_send.at[k], query_recv.at[k],
            "tp", target,
        )

    for k in range(1, replicas):
        message_to(k).start()
    for p in range(pieces):
        for k in range(1, replicas):
            when(carries(lax.rem(ep + k, replicas)), lambda: chunk_to(p, k).start())

    heads, latent = query_heads.shape[1:]
    query_copy.wait()
    for h in range(heads):
        query_heads[:, h, :] = query_rows[:, h * latent : (h + 1) * latent].astype(jnp.float32)
    sent_queries[...] = query_heads[...].astype(jnp.bfloat16)
    own_queries[tp] = sent_queries[tp]
    for k in range(1, slots):
        queries_to(k).start()

    messages[ep] = message[...]
    for k in range(1, replicas):
        message_to(k).wait_recv()
    for r in range(replicas):
        tokens[r * slots : (r + 1) * slots, :] = messages[r].astype(jnp.float32)
    features[tp] = tokens[:, :width].astype(jnp.bfloat16)

    def features_to(k):
        return remote(
            features.at[tp], features.at[tp], feature_send.at[k], feature_recv.at[k],
            "tp", lax.rem(tp + k, slots),
        )

    for k in range(1, slots):
        features_to(k).start()

    def ordered_to(p, k):
        target = lax.rem(ep + k, replicas)
        return remote(
            ordered.at[target, part(p)], moved.at[rows(ep, p)],
            ordered_send.at[p, k], ordered_recv.at[p, k], "ep", target,
        )

    def root_of(target):
        root = jnp.int32(0)
        for o in range(replicas):
            root = jnp.where(plan[o, tp] == target, jnp.int32(o), root)
        return root

    def reorder(p):
        for k in range(1, replicas):
            chunk_to(p, k).wait_recv()
        for k in range(1, replicas):
            target = lax.rem(ep + k, replicas)
            ordered[target, part(p), :] = spread[p][root_of(target)]
            ordered_to(p, k).start()
        moved[rows(ep, p), :] = spread[p][root_of(ep)]

    all_weights = tokens[:, width:]
    all_lanes = lax.broadcasted_iota(jnp.int32, all_weights.shape, 1)
    weighted = []

    def raise_tokens(j):
        raised = None
        for t in range(slots):
            term = jnp.dot(
                features[t],
                up_block[j, t * width : (t + 1) * width, :],
                preferred_element_type=jnp.float32,
            )
            raised = term if raised is None else raised + term
        hidden = (raised / (1.0 + jnp.exp(-raised))).astype(jnp.bfloat16).astype(jnp.float32)
        column = jnp.sum(
            jnp.where(all_lanes == ep * experts_local + j, all_weights, 0.0), axis=1, keepdims=True
        )
        weighted.append((hidden * column).astype(jnp.bfloat16))

    for p in range(pieces):
        own_chunk[p].wait()
        when(carries(ep), lambda: reorder(p))
        if p == 0:
            for k in range(1, slots):
                features_to(k).wait_recv()
            up_copy.wait()
        if p < experts_local and p < pieces - 1:
            raise_tokens(p)
    for j in range(len(weighted), experts_local):
        raise_tokens(j)
    down_copy.wait()
    for t in range(slots):
        total = None
        for j in range(experts_local):
            term = jnp.dot(
                weighted[j],
                down_block[j, :, t * width : (t + 1) * width],
                preferred_element_type=jnp.float32,
            )
            total = term if total is None else total + term
        partials[t] = total.astype(jnp.bfloat16)

    def partial_to(k):
        target = lax.rem(tp + k, slots)
        return remote(
            partials.at[target], arrived.at[tp], partial_send.at[k], partial_recv.at[k],
            "tp", target,
        )

    for k in range(1, slots):
        partial_to(k).start()

    totals[...] = partials[tp].astype(jnp.float32)
    for k in range(1, slots):
        partial_to(k).wait_recv()
        totals[...] += arrived[lax.rem(tp + slots - k, slots)].astype(jnp.float32)
    for r in range(replicas):
        shares[r] = totals[r * slots : (r + 1) * slots, :].astype(jnp.bfloat16)

    def share_to(k):
        target = lax.rem(ep + k, replicas)
        return remote(
            shares.at[target], returned.at[ep], share_send.at[k], share_recv.at[k],
            "ep", target,
        )

    for k in range(1, slots):
        queries_to(k).wait_recv()
    for p in range(pieces):
        for k in range(1, replicas):
            source = lax.rem(ep + replicas - k, replicas)
            arrival = remote(
                ordered.at[0, part(p)], moved.at[rows(source, p)],
                ordered_send.at[p, k], ordered_recv.at[p, k], "ep", source,
            )
            when(carries(source), lambda: arrival.wait_recv())
    for k in range(1, replicas):
        share_to(k).start()
    moved_copy = pltpu.make_async_copy(moved, moved_cache, local_sem.at[4])
    moved_copy.start()
    cache = moved[...]
    query_block = own_queries[...].reshape(heads_total, latent_cache.shape[0])
    scores = jnp.dot(query_block, cache, preferred_element_type=jnp.float32) * score_scale
    positions = lax.broadcasted_iota(jnp.int32, scores.shape, 1)
    scores = jnp.where(positions < lengths[tp], scores, -jnp.inf)
    highest = jnp.max(scores, axis=1, keepdims=True)
    exps = jnp.exp(scores - highest)
    probabilities = (exps / jnp.sum(exps, axis=1, keepdims=True)).astype(jnp.bfloat16)
    result = lax.dot_general(
        probabilities, cache[:LATENT, :], (((1,), (1,)), ((), ())),
        preferred_element_type=jnp.float32,
    )
    result = jnp.where(ended[tp] == 0, result, 0.0).astype(jnp.bfloat16)
    attended[...] = result.reshape(attended.shape)

    def context_to(k):
        target = lax.rem(tp + k, slots)
        return remote(
            attended.at[target], context.at[tp], context_send.at[k], context_recv.at[k],
            "tp", target,
        )

    for k in range(1, slots):
        context_to(k).start()
    own_context = pltpu.make_async_copy(attended.at[tp], context.at[tp], local_sem.at[5])
    own_context.start()

    result = shares[ep].astype(jnp.float32)
    for k in range(1, replicas):
        share_to(k).wait_recv()
        result += returned[lax.rem(ep + replicas - k, replicas)].astype(jnp.float32)
    summed[...] = result.astype(jnp.bfloat16)
    moe_copy = pltpu.make_async_copy(summed, moe_out, local_sem.at[12])
    moe_copy.start()

    for k in range(1, slots):
        context_to(k).wait_recv()
    own_context.wait()
    moved_copy.wait()
    moe_copy.wait()
    for k in range(1, replicas):
        message_to(k).wait_send()
        share_to(k).wait_send()
        for p in range(pieces):
            when(carries(lax.rem(ep + k, replicas)), lambda: chunk_to(p, k).wait_send())
            when(carries(ep), lambda: ordered_to(p, k).wait_send())
    for k in range(1, slots):
        queries_to(k).wait_send()
        features_to(k).wait_send()
        partial_to(k).wait_send()
        context_to(k).wait_send()


def write_kernel(moved, attended, moe, moved_cache, context, moe_out, sem):
    copies = [
        pltpu.make_async_copy(moved, moved_cache, sem.at[0]),
        pltpu.make_async_copy(moe, moe_out, sem.at[1]),
    ]
    for copy in copies:
        copy.start()
    rows = attended[...].astype(jnp.float32)
    for h in range(rows.shape[1]):
        context[:, h * LATENT : (h + 1) * LATENT] = rows[:, h, :].astype(jnp.bfloat16)
    for copy in copies:
        copy.wait()


def shards(
    latent_cache,
    queries,
    destination,
    cache_len,
    finished,
    moe_input,
    expert_ids,
    route_weight,
    up_weight,
    down_weight,
):
    replicas = lax.axis_size("ep")
    slots = lax.axis_size("tp")
    latent_width, length = latent_cache.shape[1:]
    heads = queries.shape[1] // latent_width
    width = moe_input.shape[1]
    chunk = -(-(latent_width // replicas) // PACK) * PACK
    piece = chunk // 3 if chunk % (3 * PACK) == 0 else chunk
    pieces = chunk // piece
    everyone = replicas * slots
    bf16, f32 = jnp.bfloat16, jnp.float32
    dma = pltpu.SemaphoreType.DMA
    anywhere = pl.BlockSpec(memory_space=pl.ANY)
    far = pl.BlockSpec(memory_space=pltpu.HBM)
    near = pl.BlockSpec(memory_space=pltpu.VMEM)
    moved_cache, context, moe_out = pl.pallas_call(
        functools.partial(layer_kernel, replicas, slots, chunk, piece),
        out_shape=(
            jax.ShapeDtypeStruct((latent_width, length), bf16),
            jax.ShapeDtypeStruct((slots, heads, LATENT), bf16),
            jax.ShapeDtypeStruct((slots, width), bf16),
        ),
        in_specs=[far] * 10,
        out_specs=(anywhere, anywhere, anywhere),
        scratch_shapes=[
            pltpu.SMEM(destination.shape, jnp.int32),
            pltpu.SMEM(cache_len.shape, jnp.int32),
            pltpu.SMEM(finished.shape, jnp.int32),
            pltpu.VMEM(moe_input.shape, bf16),
            pltpu.VMEM(expert_ids.shape, jnp.int32),
            pltpu.VMEM(route_weight.shape, bf16),
            pltpu.VMEM(up_weight.shape, bf16),
            pltpu.VMEM(down_weight.shape, bf16),
            pltpu.VMEM((slots, width + LANES), bf16),
            pltpu.VMEM((replicas, slots, width + LANES), bf16),
            pltpu.VMEM((everyone, width + LANES), f32),
            pltpu.VMEM((slots, everyone, width), bf16),
            [pltpu.VMEM((replicas, piece, length), bf16)] * pieces,
            pltpu.VMEM((replicas, chunk, length), bf16),
            pltpu.VMEM((latent_width, length), bf16),
            pltpu.VMEM(queries.shape, bf16),
            pltpu.VMEM((slots, heads, latent_width), f32),
            pltpu.VMEM((slots, heads, latent_width), bf16),
            pltpu.VMEM((slots, heads, latent_width), bf16),
            pltpu.VMEM((slots, heads, LATENT), bf16),
            pltpu.VMEM((slots, everyone, width), bf16),
            pltpu.VMEM((slots, everyone, width), bf16),
            pltpu.VMEM((everyone, width), f32),
            pltpu.VMEM((replicas, slots, width), bf16),
            pltpu.VMEM((replicas, slots, width), bf16),
            pltpu.VMEM((slots, width), bf16),
            dma((13,)),
            dma((pieces,)),
            dma((replicas,)),
            dma((replicas,)),
            dma((pieces, replicas)),
            dma((pieces, replicas)),
            dma((pieces, replicas)),
            dma((pieces, replicas)),
            dma((slots,)),
            dma((slots,)),
            dma((slots,)),
            dma((slots,)),
            dma((slots,)),
            dma((slots,)),
            dma((slots,)),
            dma((slots,)),
            dma((replicas,)),
            dma((replicas,)),
        ],
        compiler_params=pltpu.CompilerParams(
            collective_id=0, has_side_effects=True, vmem_limit_bytes=VMEM_BYTES
        ),
    )(
        destination,
        cache_len,
        finished,
        latent_cache.reshape(latent_width, length),
        queries,
        moe_input,
        expert_ids,
        route_weight,
        up_weight,
        down_weight,
    )
    moved_cache, context, moe_out = pl.pallas_call(
        write_kernel,
        out_shape=(
            jax.ShapeDtypeStruct((latent_width, length), bf16),
            jax.ShapeDtypeStruct((slots, heads * LATENT), bf16),
            jax.ShapeDtypeStruct((slots, width), bf16),
        ),
        in_specs=[anywhere, near, anywhere],
        out_specs=(far, near, far),
        scratch_shapes=[dma((2,))],
        compiler_params=pltpu.CompilerParams(vmem_limit_bytes=VMEM_BYTES),
    )(moved_cache, context, moe_out)
    return moved_cache.reshape(1, latent_width, length), context, moe_out


def solution(mesh):
    return jax.shard_map(
        shards,
        mesh=mesh,
        in_specs=(
            P(("groups", "ep", "tp"), None, None),
            P(("groups", "ep"), "tp"),
            P("groups", None),
            P(("groups", "ep")),
            P(("groups", "ep")),
            P(("groups", "ep"), "tp"),
            P(("groups", "ep"), None),
            P(("groups", "ep"), None),
            P("ep", None, "tp"),
            P("ep", "tp", None),
        ),
        out_specs=(
            P(("groups", "ep", "tp"), None, None),
            P(("groups", "ep"), "tp"),
            P(("groups", "ep"), "tp"),
        ),
        check_vma=False,
    )
```

```python
import functools

import jax
import jax.numpy as jnp
from jax import lax
from jax.experimental import pallas as pl
from jax.experimental.pallas import tpu as pltpu
from jax.sharding import PartitionSpec as P

MESH = pl.DeviceIdType.MESH
LATENT = 512
LANES = 128
PACK = 16
VMEM_BYTES = 56 * 1024 * 1024

score_scale = 192.0 ** (-0.5)


def when(condition, body):
    if condition is None:
        body()
    else:
        pl.when(condition)(body)


def layer_kernel(
    replicas,
    slots,
    chunk,
    piece,
    destination,
    cache_len,
    finished,
    latent_cache,
    queries,
    moe_input,
    expert_ids,
    route_weight,
    up_weight,
    down_weight,
    moved_cache,
    context,
    moe_out,
    plan,
    lengths,
    ended,
    input_block,
    id_block,
    route_block,
    up_block,
    down_block,
    message,
    messages,
    tokens,
    features,
    spread,
    ordered,
    moved,
    query_rows,
    query_heads,
    sent_queries,
    own_queries,
    attended,
    partials,
    arrived,
    totals,
    shares,
    returned,
    summed,
    local_sem,
    own_sem,
    message_send,
    message_recv,
    spread_send,
    spread_recv,
    ordered_send,
    ordered_recv,
    feature_send,
    feature_recv,
    query_send,
    query_recv,
    context_send,
    context_recv,
    partial_send,
    partial_recv,
    share_send,
    share_recv,
):
    ep = lax.axis_index("ep")
    tp = lax.axis_index("tp")
    width = moe_input.shape[1]
    experts_local = up_weight.shape[0]
    carriers = latent_cache.shape[0] // chunk
    pieces = chunk // piece
    heads_total = own_queries.shape[0] * own_queries.shape[1]

    def carries(i):
        return None if carriers == replicas else i < carriers

    def forth(axis, me, count, k):
        return lax.rem(me + k, count)

    def back(axis, me, count, k):
        return lax.rem(me + count - k, count)

    def rows(i, p):
        return pl.ds(pl.multiple_of(i * chunk + p * piece, PACK), piece)

    def part(p):
        return pl.ds(p * piece, piece)

    def remote(src, dst, send, recv, axis, target):
        return pltpu.make_async_remote_copy(
            src_ref=src,
            dst_ref=dst,
            send_sem=send,
            recv_sem=recv,
            device_id={axis: target},
            device_id_type=MESH,
        )

    barrier = pltpu.get_barrier_semaphore()
    for k in range(1, replicas):
        pl.semaphore_signal(
            barrier, inc=1, device_id={"ep": lax.rem(ep + k, replicas)}, device_id_type=MESH
        )
    for k in range(1, slots):
        pl.semaphore_signal(
            barrier, inc=1, device_id={"tp": lax.rem(tp + k, slots)}, device_id_type=MESH
        )

    up_copy = pltpu.make_async_copy(up_weight, up_block, local_sem.at[0])
    down_copy = pltpu.make_async_copy(down_weight, down_block, local_sem.at[1])
    query_copy = pltpu.make_async_copy(queries, query_rows, local_sem.at[2])
    own_chunk = [
        pltpu.make_async_copy(
            latent_cache.at[rows(ep if carriers == replicas else lax.rem(ep, carriers), p)],
            spread[p].at[ep],
            own_sem.at[p],
        )
        for p in range(pieces)
    ]
    small = [
        pltpu.make_async_copy(src, dst, local_sem.at[6 + i])
        for i, (src, dst) in enumerate(
            (
                (moe_input, input_block),
                (expert_ids, id_block),
                (route_weight, route_block),
                (finished, ended),
                (destination, plan),
                (cache_len, lengths),
            )
        )
    ]
    for copy in small:
        copy.start()
    query_copy.start()
    for copy in own_chunk:
        copy.start()

    lane = lax.broadcasted_iota(jnp.int32, (slots, LANES), 1)
    token = lax.broadcasted_iota(jnp.int32, (slots, LANES), 0)
    table = jnp.zeros((slots, LANES), jnp.float32)
    for copy in small:
        copy.wait()
    ids = id_block[...]
    weights = route_block[...].astype(jnp.float32)
    for k in range(ids.shape[1]):
        table += jnp.where(ids[:, k : k + 1] == lane, weights[:, k : k + 1], 0.0)
    for s in range(slots):
        table = jnp.where((token == s) & (ended[s] != 0), 0.0, table)
    message[:, :width] = input_block[...]
    message[:, width:] = table.astype(jnp.bfloat16)

    pl.semaphore_wait(barrier, replicas + slots - 2)

    up_copy.start()
    down_copy.start()

    def message_to(k):
        return remote(
            message, messages.at[ep], message_send.at[k], message_recv.at[k],
            "ep", lax.rem(ep + k, replicas),
        )

    def chunk_to(p, k):
        target = lax.rem(ep + k, replicas)
        return remote(
            latent_cache.at[rows(target, p)], spread[p].at[ep],
            spread_send.at[p, k], spread_recv.at[p, k], "ep", target,
        )

    def queries_to(k):
        target = lax.rem(tp + k, slots)
        return remote(
            sent_queries.at[target], own_queries.at[tp], query_send.at[k], query_recv.at[k],
            "tp", target,
        )

    for k in range(1, replicas):
        message_to(k).start()
    for p in range(pieces):
        for k in range(1, replicas):
            when(carries(lax.rem(ep + k, replicas)), lambda: chunk_to(p, k).start())

    heads, latent = query_heads.shape[1:]
    query_copy.wait()
    for h in range(heads):
        query_heads[:, h, :] = query_rows[:, h * latent : (h + 1) * latent].astype(jnp.float32)
    sent_queries[...] = query_heads[...].astype(jnp.bfloat16)
    own_queries[tp] = sent_queries[tp]
    for k in range(1, slots):
        queries_to(k).start()

    messages[ep] = message[...]
    for k in range(1, replicas):
        message_to(k).wait_recv()
    for r in range(replicas):
        tokens[r * slots : (r + 1) * slots, :] = messages[r].astype(jnp.float32)
    features[tp] = tokens[:, :width].astype(jnp.bfloat16)

    def features_to(k):
        return remote(
            features.at[tp], features.at[tp], feature_send.at[k], feature_recv.at[k],
            "tp", lax.rem(tp + k, slots),
        )

    for k in range(1, slots):
        features_to(k).start()

    def ordered_to(p, k):
        target = lax.rem(ep + k, replicas)
        return remote(
            ordered.at[target, part(p)], moved.at[rows(ep, p)],
            ordered_send.at[p, k], ordered_recv.at[p, k], "ep", target,
        )

    def root_of(target):
        root = jnp.int32(0)
        for o in range(replicas):
            root = jnp.where(plan[o, tp] == target, jnp.int32(o), root)
        return root

    def reorder(p):
        for k in range(1, replicas):
            chunk_to(p, k).wait_recv()
        for k in range(1, replicas):
            target = lax.rem(ep + k, replicas)
            ordered[target, part(p), :] = spread[p][root_of(target)]
            ordered_to(p, k).start()
        moved[rows(ep, p), :] = spread[p][root_of(ep)]

    all_weights = tokens[:, width:]
    all_lanes = lax.broadcasted_iota(jnp.int32, all_weights.shape, 1)
    weighted = []

    def raise_tokens(j):
        raised = None
        for t in range(slots):
            term = jnp.dot(
                features[t],
                up_block[j, t * width : (t + 1) * width, :],
                preferred_element_type=jnp.float32,
            )
            raised = term if raised is None else raised + term
        hidden = (raised / (1.0 + jnp.exp(-raised))).astype(jnp.bfloat16).astype(jnp.float32)
        column = jnp.sum(
            jnp.where(all_lanes == ep * experts_local + j, all_weights, 0.0), axis=1, keepdims=True
        )
        weighted.append((hidden * column).astype(jnp.bfloat16))

    for p in range(pieces):
        own_chunk[p].wait()
        when(carries(ep), lambda: reorder(p))
        if p == 0:
            for k in range(1, slots):
                features_to(k).wait_recv()
            up_copy.wait()
        if p < experts_local and p < pieces - 1:
            raise_tokens(p)
    for j in range(len(weighted), experts_local):
        raise_tokens(j)
    down_copy.wait()
    for t in range(slots):
        total = None
        for j in range(experts_local):
            term = jnp.dot(
                weighted[j],
                down_block[j, :, t * width : (t + 1) * width],
                preferred_element_type=jnp.float32,
            )
            total = term if total is None else total + term
        partials[t] = total.astype(jnp.bfloat16)

    def partial_to(k):
        target = lax.rem(tp + k, slots)
        return remote(
            partials.at[target], arrived.at[tp], partial_send.at[k], partial_recv.at[k],
            "tp", target,
        )

    for k in range(1, slots):
        partial_to(k).start()

    totals[...] = partials[tp].astype(jnp.float32)
    for k in range(1, slots):
        partial_to(k).wait_recv()
        totals[...] += arrived[lax.rem(tp + slots - k, slots)].astype(jnp.float32)
    for r in range(replicas):
        shares[r] = totals[r * slots : (r + 1) * slots, :].astype(jnp.bfloat16)

    def share_to(k):
        target = lax.rem(ep + k, replicas)
        return remote(
            shares.at[target], returned.at[ep], share_send.at[k], share_recv.at[k],
            "ep", target,
        )

    for k in range(1, slots):
        queries_to(k).wait_recv()
    for p in range(pieces):
        for k in range(1, replicas):
            source = lax.rem(ep + replicas - k, replicas)
            arrival = remote(
                ordered.at[0, part(p)], moved.at[rows(source, p)],
                ordered_send.at[p, k], ordered_recv.at[p, k], "ep", source,
            )
            when(carries(source), lambda: arrival.wait_recv())
    for k in range(1, replicas):
        share_to(k).start()
    moved_copy = pltpu.make_async_copy(moved, moved_cache, local_sem.at[4])
    moved_copy.start()
    cache = moved[...]
    query_block = own_queries[...].reshape(heads_total, latent_cache.shape[0])
    scores = jnp.dot(query_block, cache, preferred_element_type=jnp.float32) * score_scale
    positions = lax.broadcasted_iota(jnp.int32, scores.shape, 1)
    scores = jnp.where(positions < lengths[tp], scores, -jnp.inf)
    highest = jnp.max(scores, axis=1, keepdims=True)
    exps = jnp.exp(scores - highest)
    probabilities = (exps / jnp.sum(exps, axis=1, keepdims=True)).astype(jnp.bfloat16)
    result = lax.dot_general(
        probabilities, cache[:LATENT, :], (((1,), (1,)), ((), ())),
        preferred_element_type=jnp.float32,
    )
    result = jnp.where(ended[tp] == 0, result, 0.0).astype(jnp.bfloat16)
    attended[...] = result.reshape(attended.shape)

    def context_to(k):
        target = lax.rem(tp + k, slots)
        return remote(
            attended.at[target], context.at[tp], context_send.at[k], context_recv.at[k],
            "tp", target,
        )

    for k in range(1, slots):
        context_to(k).start()
    own_context = pltpu.make_async_copy(attended.at[tp], context.at[tp], local_sem.at[5])
    own_context.start()

    result = shares[ep].astype(jnp.float32)
    for k in range(1, replicas):
        share_to(k).wait_recv()
        result += returned[lax.rem(ep + replicas - k, replicas)].astype(jnp.float32)
    summed[...] = result.astype(jnp.bfloat16)
    moe_copy = pltpu.make_async_copy(summed, moe_out, local_sem.at[12])
    moe_copy.start()

    for k in range(1, slots):
        context_to(k).wait_recv()
    own_context.wait()
    moved_copy.wait()
    moe_copy.wait()
    for k in range(1, replicas):
        message_to(k).wait_send()
        share_to(k).wait_send()
        for p in range(pieces):
            when(carries(lax.rem(ep + k, replicas)), lambda: chunk_to(p, k).wait_send())
            when(carries(ep), lambda: ordered_to(p, k).wait_send())
    for k in range(1, slots):
        queries_to(k).wait_send()
        features_to(k).wait_send()
        partial_to(k).wait_send()
        context_to(k).wait_send()


def write_kernel(
    moved, attended, moe, moved_cache, context, moe_out, cache_block, rows_block, moe_block, line_block, sem
):
    parts = moved.shape[0] // 144
    cuts = [pl.ds(i * 144, 144) for i in range(parts)]
    rows_in = pltpu.make_async_copy(attended, rows_block, sem.at[0])
    rows_out = pltpu.make_async_copy(line_block, context, sem.at[1])
    moe_in = pltpu.make_async_copy(moe, moe_block, sem.at[2])
    moe_back = pltpu.make_async_copy(moe_block, moe_out, sem.at[3])
    cache_in = [
        pltpu.make_async_copy(moved.at[cut], cache_block.at[cut], sem.at[4 + i])
        for i, cut in enumerate(cuts)
    ]
    cache_out = [
        pltpu.make_async_copy(cache_block.at[cut], moved_cache.at[cut], sem.at[4 + parts + i])
        for i, cut in enumerate(cuts)
    ]
    for copy in [rows_in] + cache_in + [moe_in]:
        copy.start()
    rows_in.wait()
    rows = rows_block[...].astype(jnp.float32)
    for h in range(rows.shape[1]):
        line_block[:, h * LATENT : (h + 1) * LATENT] = rows[:, h, :].astype(jnp.bfloat16)
    rows_out.start()
    for arrived, leaving in zip(cache_in, cache_out):
        arrived.wait()
        leaving.start()
    moe_in.wait()
    moe_back.start()
    for copy in cache_out + [rows_out, moe_back]:
        copy.wait()


def shards(
    latent_cache,
    queries,
    destination,
    cache_len,
    finished,
    moe_input,
    expert_ids,
    route_weight,
    up_weight,
    down_weight,
):
    replicas = lax.axis_size("ep")
    slots = lax.axis_size("tp")
    latent_width, length = latent_cache.shape[1:]
    heads = queries.shape[1] // latent_width
    width = moe_input.shape[1]
    chunk = -(-(latent_width // replicas) // PACK) * PACK
    piece = chunk // 3 if chunk % (3 * PACK) == 0 else chunk
    pieces = chunk // piece
    everyone = replicas * slots
    bf16, f32 = jnp.bfloat16, jnp.float32
    dma = pltpu.SemaphoreType.DMA
    anywhere = pl.BlockSpec(memory_space=pl.ANY)
    far = pl.BlockSpec(memory_space=pltpu.HBM)
    moved_cache, context, moe_out = pl.pallas_call(
        functools.partial(layer_kernel, replicas, slots, chunk, piece),
        out_shape=(
            jax.ShapeDtypeStruct((latent_width, length), bf16),
            jax.ShapeDtypeStruct((slots, heads, LATENT), bf16),
            jax.ShapeDtypeStruct((slots, width), bf16),
        ),
        in_specs=[far] * 10,
        out_specs=(anywhere, anywhere, anywhere),
        scratch_shapes=[
            pltpu.SMEM(destination.shape, jnp.int32),
            pltpu.SMEM(cache_len.shape, jnp.int32),
            pltpu.SMEM(finished.shape, jnp.int32),
            pltpu.VMEM(moe_input.shape, bf16),
            pltpu.VMEM(expert_ids.shape, jnp.int32),
            pltpu.VMEM(route_weight.shape, bf16),
            pltpu.VMEM(up_weight.shape, bf16),
            pltpu.VMEM(down_weight.shape, bf16),
            pltpu.VMEM((slots, width + LANES), bf16),
            pltpu.VMEM((replicas, slots, width + LANES), bf16),
            pltpu.VMEM((everyone, width + LANES), f32),
            pltpu.VMEM((slots, everyone, width), bf16),
            [pltpu.VMEM((replicas, piece, length), bf16)] * pieces,
            pltpu.VMEM((replicas, chunk, length), bf16),
            pltpu.VMEM((latent_width, length), bf16),
            pltpu.VMEM(queries.shape, bf16),
            pltpu.VMEM((slots, heads, latent_width), f32),
            pltpu.VMEM((slots, heads, latent_width), bf16),
            pltpu.VMEM((slots, heads, latent_width), bf16),
            pltpu.VMEM((slots, heads, LATENT), bf16),
            pltpu.VMEM((slots, everyone, width), bf16),
            pltpu.VMEM((slots, everyone, width), bf16),
            pltpu.VMEM((everyone, width), f32),
            pltpu.VMEM((replicas, slots, width), bf16),
            pltpu.VMEM((replicas, slots, width), bf16),
            pltpu.VMEM((slots, width), bf16),
            dma((13,)),
            dma((pieces,)),
            dma((replicas,)),
            dma((replicas,)),
            dma((pieces, replicas)),
            dma((pieces, replicas)),
            dma((pieces, replicas)),
            dma((pieces, replicas)),
            dma((slots,)),
            dma((slots,)),
            dma((slots,)),
            dma((slots,)),
            dma((slots,)),
            dma((slots,)),
            dma((slots,)),
            dma((slots,)),
            dma((replicas,)),
            dma((replicas,)),
        ],
        compiler_params=pltpu.CompilerParams(
            collective_id=0, has_side_effects=True, vmem_limit_bytes=VMEM_BYTES
        ),
    )(
        destination,
        cache_len,
        finished,
        latent_cache.reshape(latent_width, length),
        queries,
        moe_input,
        expert_ids,
        route_weight,
        up_weight,
        down_weight,
    )
    moved_cache, context, moe_out = pl.pallas_call(
        write_kernel,
        out_shape=(
            jax.ShapeDtypeStruct((latent_width, length), bf16),
            jax.ShapeDtypeStruct((slots, heads * LATENT), bf16),
            jax.ShapeDtypeStruct((slots, width), bf16),
        ),
        in_specs=[anywhere] * 3,
        out_specs=(far, far, far),
        scratch_shapes=[
            pltpu.VMEM((latent_width, length), bf16),
            pltpu.VMEM((slots, heads, LATENT), bf16),
            pltpu.VMEM((slots, width), bf16),
            pltpu.VMEM((slots, heads * LATENT), bf16),
            dma((4 + 2 * (latent_width // 144),)),
        ],
        compiler_params=pltpu.CompilerParams(vmem_limit_bytes=VMEM_BYTES),
    )(moved_cache, context, moe_out)
    return moved_cache.reshape(1, latent_width, length), context, moe_out


def solution(mesh):
    return jax.shard_map(
        shards,
        mesh=mesh,
        in_specs=(
            P(("groups", "ep", "tp"), None, None),
            P(("groups", "ep"), "tp"),
            P("groups", None),
            P(("groups", "ep")),
            P(("groups", "ep")),
            P(("groups", "ep"), "tp"),
            P(("groups", "ep"), None),
            P(("groups", "ep"), None),
            P("ep", None, "tp"),
            P("ep", "tp", None),
        ),
        out_specs=(
            P(("groups", "ep", "tp"), None, None),
            P(("groups", "ep"), "tp"),
            P(("groups", "ep"), "tp"),
        ),
        check_vma=False,
    )
```

```python
import functools

import jax
import jax.numpy as jnp
from jax import lax
from jax.experimental import pallas as pl
from jax.experimental.pallas import tpu as pltpu
from jax.sharding import PartitionSpec as P

MESH = pl.DeviceIdType.MESH
LATENT = 512
LANES = 128
PACK = 16
PIECES = 3
WINDOW = 3
VMEM_BYTES = 56 * 1024 * 1024

score_scale = 192.0 ** (-0.5)


def when(condition, body):
    if condition is None:
        body()
    else:
        pl.when(condition)(body)


def forth(me, count, k):
    if count & (count - 1):
        return lax.rem(me + k, count)
    other, bit = me, 1
    while bit < count:
        if k & bit:
            other = other + bit - 2 * bit * lax.rem(lax.div(me, bit), 2)
        bit *= 2
    return other


def back(me, count, k):
    return lax.rem(me + count - k, count) if count & (count - 1) else forth(me, count, k)


def hops(count):
    return list(range(count // 2, count)) + list(range(1, count // 2))


def layer_kernel(
    replicas,
    slots,
    chunk,
    piece,
    destination,
    cache_len,
    finished,
    latent_cache,
    queries,
    moe_input,
    expert_ids,
    route_weight,
    up_weight,
    down_weight,
    moved_cache,
    context,
    moe_out,
    plan,
    lengths,
    ended,
    input_block,
    id_block,
    route_block,
    up_block,
    down_block,
    message,
    messages,
    tokens,
    features,
    spread,
    ordered,
    moved,
    query_rows,
    query_heads,
    sent_queries,
    own_queries,
    attended,
    partials,
    arrived,
    totals,
    shares,
    returned,
    summed,
    local_sem,
    own_sem,
    message_send,
    message_recv,
    spread_send,
    spread_recv,
    ordered_send,
    ordered_recv,
    feature_send,
    feature_recv,
    query_send,
    query_recv,
    context_send,
    context_recv,
    partial_send,
    partial_recv,
    share_send,
    share_recv,
):
    ep = lax.axis_index("ep")
    tp = lax.axis_index("tp")
    width = moe_input.shape[1]
    experts_local = up_weight.shape[0]
    carriers = latent_cache.shape[0] // chunk
    pieces = chunk // piece
    heads_total = own_queries.shape[0] * own_queries.shape[1]

    def carries(i):
        return None if carriers == replicas else i < carriers

    def rows(i, p):
        return pl.ds(pl.multiple_of(i * chunk + p * piece, PACK), piece)

    def part(p):
        return pl.ds(p * piece, piece)

    def remote(src, dst, send, recv, axis, target):
        return pltpu.make_async_remote_copy(
            src_ref=src,
            dst_ref=dst,
            send_sem=send,
            recv_sem=recv,
            device_id={axis: target},
            device_id_type=MESH,
        )

    barrier = pltpu.get_barrier_semaphore()
    for k in hops(replicas):
        pl.semaphore_signal(
            barrier, inc=1, device_id={"ep": forth(ep, replicas, k)}, device_id_type=MESH
        )
    for k in hops(slots):
        pl.semaphore_signal(
            barrier, inc=1, device_id={"tp": forth(tp, slots, k)}, device_id_type=MESH
        )

    up_copy = pltpu.make_async_copy(up_weight, up_block, local_sem.at[0])
    down_copy = pltpu.make_async_copy(down_weight, down_block, local_sem.at[1])
    query_copy = pltpu.make_async_copy(queries, query_rows, local_sem.at[2])
    own_chunk = [
        pltpu.make_async_copy(
            latent_cache.at[rows(ep if carriers == replicas else lax.rem(ep, carriers), p)],
            spread[p].at[ep],
            own_sem.at[p],
        )
        for p in range(pieces)
    ]
    small = [
        pltpu.make_async_copy(src, dst, local_sem.at[6 + i])
        for i, (src, dst) in enumerate(
            (
                (moe_input, input_block),
                (expert_ids, id_block),
                (route_weight, route_block),
                (finished, ended),
                (destination, plan),
                (cache_len, lengths),
            )
        )
    ]
    for copy in small:
        copy.start()
    query_copy.start()
    for copy in own_chunk:
        copy.start()

    lane = lax.broadcasted_iota(jnp.int32, (slots, LANES), 1)
    token = lax.broadcasted_iota(jnp.int32, (slots, LANES), 0)
    table = jnp.zeros((slots, LANES), jnp.float32)
    for copy in small:
        copy.wait()
    ids = id_block[...]
    weights = route_block[...].astype(jnp.float32)
    for k in range(ids.shape[1]):
        table += jnp.where(ids[:, k : k + 1] == lane, weights[:, k : k + 1], 0.0)
    for s in range(slots):
        table = jnp.where((token == s) & (ended[s] != 0), 0.0, table)
    message[:, :width] = input_block[...]
    message[:, width:] = table.astype(jnp.bfloat16)

    pl.semaphore_wait(barrier, replicas + slots - 2)

    up_copy.start()
    down_copy.start()

    def message_to(k):
        return remote(
            message, messages.at[ep], message_send.at[k], message_recv.at[k],
            "ep", forth(ep, replicas, k),
        )

    def chunk_to(p, k):
        target = forth(ep, replicas, k)
        return remote(
            latent_cache.at[rows(target, p)], spread[p].at[ep],
            spread_send.at[p, k], spread_recv.at[p, k], "ep", target,
        )

    def queries_to(k):
        target = forth(tp, slots, k)
        return remote(
            sent_queries.at[target], own_queries.at[tp], query_send.at[k], query_recv.at[k],
            "tp", target,
        )

    for k in hops(replicas):
        message_to(k).start()
    def send_piece(p):
        for k in hops(replicas):
            when(carries(forth(ep, replicas, k)), lambda: chunk_to(p, k).start())

    for p in range(min(WINDOW, pieces)):
        send_piece(p)

    heads, latent = query_heads.shape[1:]
    query_copy.wait()
    for h in range(heads):
        query_heads[:, h, :] = query_rows[:, h * latent : (h + 1) * latent].astype(jnp.float32)
    sent_queries[...] = query_heads[...].astype(jnp.bfloat16)
    own_queries[tp] = sent_queries[tp]
    for k in hops(slots):
        queries_to(k).start()

    messages[ep] = message[...]
    for k in hops(replicas):
        message_to(k).wait_recv()
    for r in range(replicas):
        tokens[r * slots : (r + 1) * slots, :] = messages[r].astype(jnp.float32)
    features[tp] = tokens[:, :width].astype(jnp.bfloat16)

    def features_to(k):
        return remote(
            features.at[tp], features.at[tp], feature_send.at[k], feature_recv.at[k],
            "tp", forth(tp, slots, k),
        )

    for k in hops(slots):
        features_to(k).start()

    def ordered_to(p, k):
        target = forth(ep, replicas, k)
        return remote(
            ordered.at[target, part(p)], moved.at[rows(ep, p)],
            ordered_send.at[p, k], ordered_recv.at[p, k], "ep", target,
        )

    def root_of(target):
        root = jnp.int32(0)
        for o in range(replicas):
            root = jnp.where(plan[o, tp] == target, jnp.int32(o), root)
        return root

    def reorder(p):
        for k in hops(replicas):
            chunk_to(p, k).wait_recv()
        for k in hops(replicas):
            target = forth(ep, replicas, k)
            ordered[target, part(p), :] = spread[p][root_of(target)]
            ordered_to(p, k).start()
        moved[rows(ep, p), :] = spread[p][root_of(ep)]

    all_weights = tokens[:, width:]
    all_lanes = lax.broadcasted_iota(jnp.int32, all_weights.shape, 1)
    weighted = []

    def raise_tokens(j):
        raised = None
        for t in range(slots):
            term = jnp.dot(
                features[t],
                up_block[j, t * width : (t + 1) * width, :],
                preferred_element_type=jnp.float32,
            )
            raised = term if raised is None else raised + term
        hidden = (raised / (1.0 + jnp.exp(-raised))).astype(jnp.bfloat16).astype(jnp.float32)
        column = jnp.sum(
            jnp.where(all_lanes == ep * experts_local + j, all_weights, 0.0), axis=1, keepdims=True
        )
        weighted.append((hidden * column).astype(jnp.bfloat16))

    for p in range(pieces):
        own_chunk[p].wait()
        when(carries(ep), lambda: reorder(p))
        if p + WINDOW < pieces:
            send_piece(p + WINDOW)
        if p == 0:
            for k in hops(slots):
                features_to(k).wait_recv()
            up_copy.wait()
        if p < experts_local and p < pieces - 1:
            raise_tokens(p)
    for j in range(len(weighted), experts_local):
        raise_tokens(j)
    down_copy.wait()
    for t in range(slots):
        total = None
        for j in range(experts_local):
            term = jnp.dot(
                weighted[j],
                down_block[j, :, t * width : (t + 1) * width],
                preferred_element_type=jnp.float32,
            )
            total = term if total is None else total + term
        partials[t] = total.astype(jnp.bfloat16)

    def partial_to(k):
        target = forth(tp, slots, k)
        return remote(
            partials.at[target], arrived.at[tp], partial_send.at[k], partial_recv.at[k],
            "tp", target,
        )

    for k in hops(slots):
        partial_to(k).start()

    totals[...] = partials[tp].astype(jnp.float32)
    for k in hops(slots):
        partial_to(k).wait_recv()
        totals[...] += arrived[back(tp, slots, k)].astype(jnp.float32)
    for r in range(replicas):
        shares[r] = totals[r * slots : (r + 1) * slots, :].astype(jnp.bfloat16)

    def share_to(k):
        target = forth(ep, replicas, k)
        return remote(
            shares.at[target], returned.at[ep], share_send.at[k], share_recv.at[k],
            "ep", target,
        )

    for k in hops(replicas):
        share_to(k).start()

    for k in hops(slots):
        queries_to(k).wait_recv()
    for p in range(pieces):
        for k in hops(replicas):
            source = back(ep, replicas, k)
            arrival = remote(
                ordered.at[0, part(p)], moved.at[rows(source, p)],
                ordered_send.at[p, k], ordered_recv.at[p, k], "ep", source,
            )
            when(carries(source), lambda: arrival.wait_recv())
    moved_copy = pltpu.make_async_copy(moved, moved_cache, local_sem.at[4])
    moved_copy.start()
    cache = moved[...]
    query_block = own_queries[...].reshape(heads_total, latent_cache.shape[0])
    scores = jnp.dot(query_block, cache, preferred_element_type=jnp.float32) * score_scale
    positions = lax.broadcasted_iota(jnp.int32, scores.shape, 1)
    scores = jnp.where(positions < lengths[tp], scores, -jnp.inf)
    highest = jnp.max(scores, axis=1, keepdims=True)
    exps = jnp.exp(scores - highest)
    probabilities = (exps / jnp.sum(exps, axis=1, keepdims=True)).astype(jnp.bfloat16)
    result = lax.dot_general(
        probabilities, cache[:LATENT, :], (((1,), (1,)), ((), ())),
        preferred_element_type=jnp.float32,
    )
    result = jnp.where(ended[tp] == 0, result, 0.0).astype(jnp.bfloat16)
    attended[...] = result.reshape(attended.shape)

    def context_to(k):
        target = forth(tp, slots, k)
        return remote(
            attended.at[target], context.at[tp], context_send.at[k], context_recv.at[k],
            "tp", target,
        )

    for k in hops(slots):
        context_to(k).start()
    own_context = pltpu.make_async_copy(attended.at[tp], context.at[tp], local_sem.at[5])
    own_context.start()

    result = shares[ep].astype(jnp.float32)
    for k in hops(replicas):
        share_to(k).wait_recv()
        result += returned[back(ep, replicas, k)].astype(jnp.float32)
    summed[...] = result.astype(jnp.bfloat16)
    moe_copy = pltpu.make_async_copy(summed, moe_out, local_sem.at[12])
    moe_copy.start()

    for k in hops(slots):
        context_to(k).wait_recv()
    own_context.wait()
    moved_copy.wait()
    moe_copy.wait()
    for k in hops(replicas):
        message_to(k).wait_send()
        share_to(k).wait_send()
        for p in range(pieces):
            when(carries(forth(ep, replicas, k)), lambda: chunk_to(p, k).wait_send())
            when(carries(ep), lambda: ordered_to(p, k).wait_send())
    for k in hops(slots):
        queries_to(k).wait_send()
        features_to(k).wait_send()
        partial_to(k).wait_send()
        context_to(k).wait_send()


def write_kernel(
    moved, attended, moe, moved_cache, context, moe_out, cache_block, rows_block, moe_block, line_block, sem
):
    parts = moved.shape[0] // 144
    cuts = [pl.ds(i * 144, 144) for i in range(parts)]
    rows_in = pltpu.make_async_copy(attended, rows_block, sem.at[0])
    rows_out = pltpu.make_async_copy(line_block, context, sem.at[1])
    moe_in = pltpu.make_async_copy(moe, moe_block, sem.at[2])
    moe_back = pltpu.make_async_copy(moe_block, moe_out, sem.at[3])
    cache_in = [
        pltpu.make_async_copy(moved.at[cut], cache_block.at[cut], sem.at[4 + i])
        for i, cut in enumerate(cuts)
    ]
    cache_out = [
        pltpu.make_async_copy(cache_block.at[cut], moved_cache.at[cut], sem.at[4 + parts + i])
        for i, cut in enumerate(cuts)
    ]
    for copy in [rows_in] + cache_in + [moe_in]:
        copy.start()
    rows_in.wait()
    rows = rows_block[...].astype(jnp.float32)
    for h in range(rows.shape[1]):
        line_block[:, h * LATENT : (h + 1) * LATENT] = rows[:, h, :].astype(jnp.bfloat16)
    rows_out.start()
    for arrived, leaving in zip(cache_in, cache_out):
        arrived.wait()
        leaving.start()
    moe_in.wait()
    moe_back.start()
    for copy in cache_out + [rows_out, moe_back]:
        copy.wait()


def shards(
    latent_cache,
    queries,
    destination,
    cache_len,
    finished,
    moe_input,
    expert_ids,
    route_weight,
    up_weight,
    down_weight,
):
    replicas = lax.axis_size("ep")
    slots = lax.axis_size("tp")
    latent_width, length = latent_cache.shape[1:]
    heads = queries.shape[1] // latent_width
    width = moe_input.shape[1]
    chunk = -(-(latent_width // replicas) // PACK) * PACK
    piece = chunk // PIECES if chunk % (PIECES * PACK) == 0 else chunk
    pieces = chunk // piece
    everyone = replicas * slots
    bf16, f32 = jnp.bfloat16, jnp.float32
    dma = pltpu.SemaphoreType.DMA
    anywhere = pl.BlockSpec(memory_space=pl.ANY)
    far = pl.BlockSpec(memory_space=pltpu.HBM)
    moved_cache, context, moe_out = pl.pallas_call(
        functools.partial(layer_kernel, replicas, slots, chunk, piece),
        out_shape=(
            jax.ShapeDtypeStruct((latent_width, length), bf16),
            jax.ShapeDtypeStruct((slots, heads, LATENT), bf16),
            jax.ShapeDtypeStruct((slots, width), bf16),
        ),
        in_specs=[far] * 10,
        out_specs=(anywhere, anywhere, anywhere),
        scratch_shapes=[
            pltpu.SMEM(destination.shape, jnp.int32),
            pltpu.SMEM(cache_len.shape, jnp.int32),
            pltpu.SMEM(finished.shape, jnp.int32),
            pltpu.VMEM(moe_input.shape, bf16),
            pltpu.VMEM(expert_ids.shape, jnp.int32),
            pltpu.VMEM(route_weight.shape, bf16),
            pltpu.VMEM(up_weight.shape, bf16),
            pltpu.VMEM(down_weight.shape, bf16),
            pltpu.VMEM((slots, width + LANES), bf16),
            pltpu.VMEM((replicas, slots, width + LANES), bf16),
            pltpu.VMEM((everyone, width + LANES), f32),
            pltpu.VMEM((slots, everyone, width), bf16),
            [pltpu.VMEM((replicas, piece, length), bf16)] * pieces,
            pltpu.VMEM((replicas, chunk, length), bf16),
            pltpu.VMEM((latent_width, length), bf16),
            pltpu.VMEM(queries.shape, bf16),
            pltpu.VMEM((slots, heads, latent_width), f32),
            pltpu.VMEM((slots, heads, latent_width), bf16),
            pltpu.VMEM((slots, heads, latent_width), bf16),
            pltpu.VMEM((slots, heads, LATENT), bf16),
            pltpu.VMEM((slots, everyone, width), bf16),
            pltpu.VMEM((slots, everyone, width), bf16),
            pltpu.VMEM((everyone, width), f32),
            pltpu.VMEM((replicas, slots, width), bf16),
            pltpu.VMEM((replicas, slots, width), bf16),
            pltpu.VMEM((slots, width), bf16),
            dma((13,)),
            dma((pieces,)),
            dma((replicas,)),
            dma((replicas,)),
            dma((pieces, replicas)),
            dma((pieces, replicas)),
            dma((pieces, replicas)),
            dma((pieces, replicas)),
            dma((slots,)),
            dma((slots,)),
            dma((slots,)),
            dma((slots,)),
            dma((slots,)),
            dma((slots,)),
            dma((slots,)),
            dma((slots,)),
            dma((replicas,)),
            dma((replicas,)),
        ],
        compiler_params=pltpu.CompilerParams(
            collective_id=0, has_side_effects=True, vmem_limit_bytes=VMEM_BYTES
        ),
    )(
        destination,
        cache_len,
        finished,
        latent_cache.reshape(latent_width, length),
        queries,
        moe_input,
        expert_ids,
        route_weight,
        up_weight,
        down_weight,
    )
    moved_cache, context, moe_out = pl.pallas_call(
        write_kernel,
        out_shape=(
            jax.ShapeDtypeStruct((latent_width, length), bf16),
            jax.ShapeDtypeStruct((slots, heads * LATENT), bf16),
            jax.ShapeDtypeStruct((slots, width), bf16),
        ),
        in_specs=[anywhere] * 3,
        out_specs=(far, far, far),
        scratch_shapes=[
            pltpu.VMEM((latent_width, length), bf16),
            pltpu.VMEM((slots, heads, LATENT), bf16),
            pltpu.VMEM((slots, width), bf16),
            pltpu.VMEM((slots, heads * LATENT), bf16),
            dma((4 + 2 * (latent_width // 144),)),
        ],
        compiler_params=pltpu.CompilerParams(vmem_limit_bytes=VMEM_BYTES),
    )(moved_cache, context, moe_out)
    return moved_cache.reshape(1, latent_width, length), context, moe_out


def solution(mesh):
    return jax.shard_map(
        shards,
        mesh=mesh,
        in_specs=(
            P(("groups", "ep", "tp"), None, None),
            P(("groups", "ep"), "tp"),
            P("groups", None),
            P(("groups", "ep")),
            P(("groups", "ep")),
            P(("groups", "ep"), "tp"),
            P(("groups", "ep"), None),
            P(("groups", "ep"), None),
            P("ep", None, "tp"),
            P("ep", "tp", None),
        ),
        out_specs=(
            P(("groups", "ep", "tp"), None, None),
            P(("groups", "ep"), "tp"),
            P(("groups", "ep"), "tp"),
        ),
        check_vma=False,
    )
```

```python
import functools

import jax
import jax.numpy as jnp
from jax import lax
from jax.experimental import pallas as pl
from jax.experimental.pallas import tpu as pltpu
from jax.sharding import PartitionSpec as P

MESH = pl.DeviceIdType.MESH
LATENT = 512
LANES = 128
PACK = 16
WINDOW = 3
VMEM_BYTES = 56 * 1024 * 1024

score_scale = 192.0 ** (-0.5)


def when(condition, body):
    if condition is None:
        body()
    else:
        pl.when(condition)(body)


def forth(me, count, k):
    if count & (count - 1):
        return lax.rem(me + k, count)
    other, bit = me, 1
    while bit < count:
        if k & bit:
            other = other + bit - 2 * bit * lax.rem(lax.div(me, bit), 2)
        bit *= 2
    return other


def back(me, count, k):
    return lax.rem(me + count - k, count) if count & (count - 1) else forth(me, count, k)


def hops(count):
    return list(range(count // 2, count)) + list(range(1, count // 2))


def layer_kernel(
    replicas,
    slots,
    chunk,
    piece,
    destination,
    cache_len,
    finished,
    latent_cache,
    queries,
    moe_input,
    expert_ids,
    route_weight,
    up_weight,
    down_weight,
    moved_cache,
    context,
    moe_out,
    plan,
    lengths,
    ended,
    input_block,
    id_block,
    route_block,
    up_block,
    down_block,
    message,
    messages,
    tokens,
    features,
    spread,
    ordered,
    moved,
    query_rows,
    query_heads,
    sent_queries,
    own_queries,
    attended,
    partials,
    arrived,
    totals,
    shares,
    returned,
    summed,
    local_sem,
    own_sem,
    message_send,
    message_recv,
    spread_send,
    spread_recv,
    ordered_send,
    ordered_recv,
    feature_send,
    feature_recv,
    query_send,
    query_recv,
    context_send,
    context_recv,
    partial_send,
    partial_recv,
    share_send,
    share_recv,
):
    ep = lax.axis_index("ep")
    tp = lax.axis_index("tp")
    width = moe_input.shape[1]
    experts_local = up_weight.shape[0]
    carriers = latent_cache.shape[0] // chunk
    pieces = len(piece)

    def carries(i):
        return None if carriers == replicas else i < carriers

    def rows(i, p):
        return pl.ds(pl.multiple_of(i * chunk + sum(piece[:p]), PACK), piece[p])

    def part(p):
        return pl.ds(sum(piece[:p]), piece[p])

    def remote(src, dst, send, recv, axis, target):
        return pltpu.make_async_remote_copy(
            src_ref=src,
            dst_ref=dst,
            send_sem=send,
            recv_sem=recv,
            device_id={axis: target},
            device_id_type=MESH,
        )

    barrier = pltpu.get_barrier_semaphore()
    for k in hops(replicas):
        pl.semaphore_signal(
            barrier, inc=1, device_id={"ep": forth(ep, replicas, k)}, device_id_type=MESH
        )
    for k in hops(slots):
        pl.semaphore_signal(
            barrier, inc=1, device_id={"tp": forth(tp, slots, k)}, device_id_type=MESH
        )

    up_copy = pltpu.make_async_copy(up_weight, up_block, local_sem.at[0])
    down_copy = pltpu.make_async_copy(down_weight, down_block, local_sem.at[1])
    query_copy = pltpu.make_async_copy(queries, query_rows, local_sem.at[2])
    own_chunk = [
        pltpu.make_async_copy(
            latent_cache.at[rows(ep if carriers == replicas else lax.rem(ep, carriers), p)],
            spread[p].at[ep],
            own_sem.at[p],
        )
        for p in range(pieces)
    ]
    small = [
        pltpu.make_async_copy(src, dst, local_sem.at[6 + i])
        for i, (src, dst) in enumerate(
            (
                (moe_input, input_block),
                (expert_ids, id_block),
                (route_weight, route_block),
                (finished, ended),
                (destination, plan),
                (cache_len, lengths),
            )
        )
    ]
    for copy in small:
        copy.start()
    query_copy.start()
    for copy in own_chunk:
        copy.start()

    lane = lax.broadcasted_iota(jnp.int32, (slots, LANES), 1)
    token = lax.broadcasted_iota(jnp.int32, (slots, LANES), 0)
    table = jnp.zeros((slots, LANES), jnp.float32)
    for copy in small:
        copy.wait()
    ids = id_block[...]
    weights = route_block[...].astype(jnp.float32)
    for k in range(ids.shape[1]):
        table += jnp.where(ids[:, k : k + 1] == lane, weights[:, k : k + 1], 0.0)
    for s in range(slots):
        table = jnp.where((token == s) & (ended[s] != 0), 0.0, table)
    message[:, :width] = input_block[...]
    message[:, width:] = table.astype(jnp.bfloat16)

    pl.semaphore_wait(barrier, replicas + slots - 2)

    up_copy.start()
    down_copy.start()

    def message_to(k):
        return remote(
            message, messages.at[ep], message_send.at[k], message_recv.at[k],
            "ep", forth(ep, replicas, k),
        )

    def chunk_to(p, k):
        target = forth(ep, replicas, k)
        return remote(
            latent_cache.at[rows(target, p)], spread[p].at[ep],
            spread_send.at[p, k], spread_recv.at[p, k], "ep", target,
        )

    def queries_to(k):
        target = forth(tp, slots, k)
        return remote(
            sent_queries.at[target], own_queries.at[tp], query_send.at[k], query_recv.at[k],
            "tp", target,
        )

    for k in hops(replicas):
        message_to(k).start()
    def send_piece(p):
        for k in hops(replicas):
            when(carries(forth(ep, replicas, k)), lambda: chunk_to(p, k).start())

    for p in range(min(WINDOW, pieces)):
        send_piece(p)

    heads, latent = query_heads.shape[1:]
    query_copy.wait()
    for h in range(heads):
        query_heads[:, h, :] = query_rows[:, h * latent : (h + 1) * latent].astype(jnp.float32)
    sent_queries[...] = query_heads[...].astype(jnp.bfloat16)
    own_queries[tp] = sent_queries[tp]
    for k in hops(slots):
        queries_to(k).start()

    messages[ep] = message[...]
    for k in hops(replicas):
        message_to(k).wait_recv()
    for r in range(replicas):
        tokens[r * slots : (r + 1) * slots, :] = messages[r].astype(jnp.float32)
    features[tp] = tokens[:, :width].astype(jnp.bfloat16)

    def features_to(k):
        return remote(
            features.at[tp], features.at[tp], feature_send.at[k], feature_recv.at[k],
            "tp", forth(tp, slots, k),
        )

    for k in hops(slots):
        features_to(k).start()

    def ordered_to(p, k):
        target = forth(ep, replicas, k)
        return remote(
            ordered.at[target, part(p)], moved.at[rows(ep, p)],
            ordered_send.at[p, k], ordered_recv.at[p, k], "ep", target,
        )

    def root_of(target):
        root = jnp.int32(0)
        for o in range(replicas):
            root = jnp.where(plan[o, tp] == target, jnp.int32(o), root)
        return root

    def reorder(p):
        for k in hops(replicas):
            chunk_to(p, k).wait_recv()
        for k in hops(replicas):
            target = forth(ep, replicas, k)
            ordered[target, part(p), :] = spread[p][root_of(target)]
            ordered_to(p, k).start()
        moved[rows(ep, p), :] = spread[p][root_of(ep)]

    all_weights = tokens[:, width:]
    all_lanes = lax.broadcasted_iota(jnp.int32, all_weights.shape, 1)
    weighted = []

    def raise_tokens(j):
        raised = None
        for t in range(slots):
            term = jnp.dot(
                features[t],
                up_block[j, t * width : (t + 1) * width, :],
                preferred_element_type=jnp.float32,
            )
            raised = term if raised is None else raised + term
        hidden = (raised / (1.0 + jnp.exp(-raised))).astype(jnp.bfloat16).astype(jnp.float32)
        column = jnp.sum(
            jnp.where(all_lanes == ep * experts_local + j, all_weights, 0.0), axis=1, keepdims=True
        )
        weighted.append((hidden * column).astype(jnp.bfloat16))

    for p in range(pieces):
        own_chunk[p].wait()
        when(carries(ep), lambda: reorder(p))
        if p + WINDOW < pieces:
            send_piece(p + WINDOW)
        if p == 0:
            for k in hops(slots):
                features_to(k).wait_recv()
            up_copy.wait()
        if p < experts_local and p < pieces - 1:
            raise_tokens(p)
    for j in range(len(weighted), experts_local):
        raise_tokens(j)
    down_copy.wait()
    for t in range(slots):
        total = None
        for j in range(experts_local):
            term = jnp.dot(
                weighted[j],
                down_block[j, :, t * width : (t + 1) * width],
                preferred_element_type=jnp.float32,
            )
            total = term if total is None else total + term
        partials[t] = total.astype(jnp.bfloat16)

    def partial_to(k):
        target = forth(tp, slots, k)
        return remote(
            partials.at[target], arrived.at[tp], partial_send.at[k], partial_recv.at[k],
            "tp", target,
        )

    for k in hops(slots):
        partial_to(k).start()

    totals[...] = partials[tp].astype(jnp.float32)
    for k in hops(slots):
        partial_to(k).wait_recv()
        totals[...] += arrived[back(tp, slots, k)].astype(jnp.float32)
    for r in range(replicas):
        shares[r] = totals[r * slots : (r + 1) * slots, :].astype(jnp.bfloat16)

    def share_to(k):
        target = forth(ep, replicas, k)
        return remote(
            shares.at[target], returned.at[ep], share_send.at[k], share_recv.at[k],
            "ep", target,
        )

    for k in hops(replicas):
        share_to(k).start()

    for k in hops(slots):
        queries_to(k).wait_recv()
    for p in range(pieces):
        for k in hops(replicas):
            source = back(ep, replicas, k)
            arrival = remote(
                ordered.at[0, part(p)], moved.at[rows(source, p)],
                ordered_send.at[p, k], ordered_recv.at[p, k], "ep", source,
            )
            when(carries(source), lambda: arrival.wait_recv())
    moved_copy = pltpu.make_async_copy(moved, moved_cache, local_sem.at[4])
    moved_copy.start()
    cache = moved[...]

    def attend(places):
        query_block = jnp.concatenate([own_queries[place] for place in places], axis=0)
        scores = jnp.dot(query_block, cache, preferred_element_type=jnp.float32) * score_scale
        positions = lax.broadcasted_iota(jnp.int32, scores.shape, 1)
        scores = jnp.where(positions < lengths[tp], scores, -jnp.inf)
        highest = jnp.max(scores, axis=1, keepdims=True)
        exps = jnp.exp(scores - highest)
        probabilities = (exps / jnp.sum(exps, axis=1, keepdims=True)).astype(jnp.bfloat16)
        result = lax.dot_general(
            probabilities, cache[:LATENT, :], (((1,), (1,)), ((), ())),
            preferred_element_type=jnp.float32,
        )
        result = jnp.where(ended[tp] == 0, result, 0.0).astype(jnp.bfloat16)
        for i, place in enumerate(places):
            attended[place] = result[i * heads : (i + 1) * heads]

    def context_to(k):
        target = forth(tp, slots, k)
        return remote(
            attended.at[target], context.at[tp], context_send.at[k], context_recv.at[k],
            "tp", target,
        )

    far_places, near_places = hops(slots)[: slots - slots // 2], hops(slots)[slots - slots // 2 :]
    attend([forth(tp, slots, k) for k in far_places])
    for k in far_places:
        context_to(k).start()
    attend([forth(tp, slots, k) for k in near_places] + [tp])
    for k in near_places:
        context_to(k).start()
    own_context = pltpu.make_async_copy(attended.at[tp], context.at[tp], local_sem.at[5])
    own_context.start()

    result = shares[ep].astype(jnp.float32)
    for k in hops(replicas):
        share_to(k).wait_recv()
        result += returned[back(ep, replicas, k)].astype(jnp.float32)
    summed[...] = result.astype(jnp.bfloat16)
    moe_copy = pltpu.make_async_copy(summed, moe_out, local_sem.at[12])
    moe_copy.start()

    for k in hops(slots):
        context_to(k).wait_recv()
    own_context.wait()
    moved_copy.wait()
    moe_copy.wait()
    for k in hops(replicas):
        message_to(k).wait_send()
        share_to(k).wait_send()
        for p in range(pieces):
            when(carries(forth(ep, replicas, k)), lambda: chunk_to(p, k).wait_send())
            when(carries(ep), lambda: ordered_to(p, k).wait_send())
    for k in hops(slots):
        queries_to(k).wait_send()
        features_to(k).wait_send()
        partial_to(k).wait_send()
        context_to(k).wait_send()


def write_kernel(
    moved, attended, moe, moved_cache, context, moe_out, cache_block, rows_block, moe_block, line_block, sem
):
    parts = moved.shape[0] // 144
    cuts = [pl.ds(i * 144, 144) for i in range(parts)]
    rows_in = pltpu.make_async_copy(attended, rows_block, sem.at[0])
    rows_out = pltpu.make_async_copy(line_block, context, sem.at[1])
    moe_in = pltpu.make_async_copy(moe, moe_block, sem.at[2])
    moe_back = pltpu.make_async_copy(moe_block, moe_out, sem.at[3])
    cache_in = [
        pltpu.make_async_copy(moved.at[cut], cache_block.at[cut], sem.at[4 + i])
        for i, cut in enumerate(cuts)
    ]
    cache_out = [
        pltpu.make_async_copy(cache_block.at[cut], moved_cache.at[cut], sem.at[4 + parts + i])
        for i, cut in enumerate(cuts)
    ]
    for copy in [rows_in] + cache_in + [moe_in]:
        copy.start()
    rows_in.wait()
    rows = rows_block[...].astype(jnp.float32)
    for h in range(rows.shape[1]):
        line_block[:, h * LATENT : (h + 1) * LATENT] = rows[:, h, :].astype(jnp.bfloat16)
    rows_out.start()
    for arrived, leaving in zip(cache_in, cache_out):
        arrived.wait()
        leaving.start()
    moe_in.wait()
    moe_back.start()
    for copy in cache_out + [rows_out, moe_back]:
        copy.wait()


def shards(
    latent_cache,
    queries,
    destination,
    cache_len,
    finished,
    moe_input,
    expert_ids,
    route_weight,
    up_weight,
    down_weight,
):
    replicas = lax.axis_size("ep")
    slots = lax.axis_size("tp")
    latent_width, length = latent_cache.shape[1:]
    heads = queries.shape[1] // latent_width
    width = moe_input.shape[1]
    chunk = -(-(latent_width // replicas) // PACK) * PACK
    units = chunk // PACK
    piece = [PACK * u for u in (units // 4, units // 3, units - units // 3 - units // 4) if u]
    pieces = len(piece)
    everyone = replicas * slots
    bf16, f32 = jnp.bfloat16, jnp.float32
    dma = pltpu.SemaphoreType.DMA
    anywhere = pl.BlockSpec(memory_space=pl.ANY)
    far = pl.BlockSpec(memory_space=pltpu.HBM)
    moved_cache, context, moe_out = pl.pallas_call(
        functools.partial(layer_kernel, replicas, slots, chunk, piece),
        out_shape=(
            jax.ShapeDtypeStruct((latent_width, length), bf16),
            jax.ShapeDtypeStruct((slots, heads, LATENT), bf16),
            jax.ShapeDtypeStruct((slots, width), bf16),
        ),
        in_specs=[far] * 10,
        out_specs=(anywhere, anywhere, anywhere),
        scratch_shapes=[
            pltpu.SMEM(destination.shape, jnp.int32),
            pltpu.SMEM(cache_len.shape, jnp.int32),
            pltpu.SMEM(finished.shape, jnp.int32),
            pltpu.VMEM(moe_input.shape, bf16),
            pltpu.VMEM(expert_ids.shape, jnp.int32),
            pltpu.VMEM(route_weight.shape, bf16),
            pltpu.VMEM(up_weight.shape, bf16),
            pltpu.VMEM(down_weight.shape, bf16),
            pltpu.VMEM((slots, width + LANES), bf16),
            pltpu.VMEM((replicas, slots, width + LANES), bf16),
            pltpu.VMEM((everyone, width + LANES), f32),
            pltpu.VMEM((slots, everyone, width), bf16),
            [pltpu.VMEM((replicas, rows, length), bf16) for rows in piece],
            pltpu.VMEM((replicas, chunk, length), bf16),
            pltpu.VMEM((latent_width, length), bf16),
            pltpu.VMEM(queries.shape, bf16),
            pltpu.VMEM((slots, heads, latent_width), f32),
            pltpu.VMEM((slots, heads, latent_width), bf16),
            pltpu.VMEM((slots, heads, latent_width), bf16),
            pltpu.VMEM((slots, heads, LATENT), bf16),
            pltpu.VMEM((slots, everyone, width), bf16),
            pltpu.VMEM((slots, everyone, width), bf16),
            pltpu.VMEM((everyone, width), f32),
            pltpu.VMEM((replicas, slots, width), bf16),
            pltpu.VMEM((replicas, slots, width), bf16),
            pltpu.VMEM((slots, width), bf16),
            dma((13,)),
            dma((pieces,)),
            dma((replicas,)),
            dma((replicas,)),
            dma((pieces, replicas)),
            dma((pieces, replicas)),
            dma((pieces, replicas)),
            dma((pieces, replicas)),
            dma((slots,)),
            dma((slots,)),
            dma((slots,)),
            dma((slots,)),
            dma((slots,)),
            dma((slots,)),
            dma((slots,)),
            dma((slots,)),
            dma((replicas,)),
            dma((replicas,)),
        ],
        compiler_params=pltpu.CompilerParams(
            collective_id=0, has_side_effects=True, vmem_limit_bytes=VMEM_BYTES
        ),
    )(
        destination,
        cache_len,
        finished,
        latent_cache.reshape(latent_width, length),
        queries,
        moe_input,
        expert_ids,
        route_weight,
        up_weight,
        down_weight,
    )
    moved_cache, context, moe_out = pl.pallas_call(
        write_kernel,
        out_shape=(
            jax.ShapeDtypeStruct((latent_width, length), bf16),
            jax.ShapeDtypeStruct((slots, heads * LATENT), bf16),
            jax.ShapeDtypeStruct((slots, width), bf16),
        ),
        in_specs=[anywhere] * 3,
        out_specs=(far, far, far),
        scratch_shapes=[
            pltpu.VMEM((latent_width, length), bf16),
            pltpu.VMEM((slots, heads, LATENT), bf16),
            pltpu.VMEM((slots, width), bf16),
            pltpu.VMEM((slots, heads * LATENT), bf16),
            dma((4 + 2 * (latent_width // 144),)),
        ],
        compiler_params=pltpu.CompilerParams(vmem_limit_bytes=VMEM_BYTES),
    )(moved_cache, context, moe_out)
    return moved_cache.reshape(1, latent_width, length), context, moe_out


def solution(mesh):
    return jax.shard_map(
        shards,
        mesh=mesh,
        in_specs=(
            P(("groups", "ep", "tp"), None, None),
            P(("groups", "ep"), "tp"),
            P("groups", None),
            P(("groups", "ep")),
            P(("groups", "ep")),
            P(("groups", "ep"), "tp"),
            P(("groups", "ep"), None),
            P(("groups", "ep"), None),
            P("ep", None, "tp"),
            P("ep", "tp", None),
        ),
        out_specs=(
            P(("groups", "ep", "tp"), None, None),
            P(("groups", "ep"), "tp"),
            P(("groups", "ep"), "tp"),
        ),
        check_vma=False,
    )
```
